256 devices in a mesh: gx: 32 (over x, y, core), gy: 8 (over z).
Axes of the slice: x: 4, y: 4, z: 8, core: 2. Of those that a mesh axis runs over, the one named last changes fastest.
Arguments:
- eastward: float32 [256, 1024, 128], P('gx', 'gy'), may hold values from -6 to 6
- northward: float32 [256, 1024, 128], P('gx', 'gy'), may hold values from -6 to 6
- vertical: float32 [256, 1024, 128], P('gx', 'gy'), may hold values from -6 to 6
- pressure: float32 [256, 1024, 128], P('gx', 'gy'), may hold values from -6 to 6
- theta: float32 [256, 1024, 128], P('gx', 'gy'), may hold values from -6 to 6
- humidity: float32 [256, 1024, 128], P('gx', 'gy'), may hold values from 0.95 to 1.07
- sound_speed: float32 [128], replicated, may hold values from 0.25 to 1
- radius_sq: float32 [64, 8, 256, 1024], P(None, None, 'gx', 'gy'), may hold values from 0.25 to 4
- multiplicity: bfloat16 [64, 8, 256, 1024], P(None, None, 'gx', 'gy'), may hold values from 0.5 to 2
- droplet_count: int32 [8, 256, 1024], P(None, 'gx', 'gy'), may hold values from 0 to 64
Outputs:
- eastward_out: float32 [256, 1024, 128], P('gx', 'gy')
- northward_out: float32 [256, 1024, 128], P('gx', 'gy')
- vertical_out: float32 [256, 1024, 128], P('gx', 'gy')
- pressure_out: float32 [256, 1024, 128], P('gx', 'gy')
- theta_out: float32 [256, 1024, 128], P('gx', 'gy')
- humidity_out: float32 [256, 1024, 128], P('gx', 'gy')
- radius_out: float32 [64, 8, 256, 1024], P(None, None, 'gx', 'gy')
- saturation_profile: float32 [128], replicated
The draws below stay inside these ranges and needn't reach their ends.
All inputs are finite; a program needn't handle non-finite values.
Results may differ from the reference program's by a relative error of at most 0.0003.
Values sent between devices are 32-bit elements; how exact they have to be, the bound alone decides.
A program may use at most 64 MiB of HBM per device.

```python
import math
import jax
import jax.numpy as jnp
from jax import lax

NZ = 128
SLOTS = 64
CLOUD = 8
SUB = 3
CLOUD_BASE = 32
NX = 256
NY = 1024


def draw_humidity(key, part):
    first, second = jax.random.split(jax.random.fold_in(key, 17))
    across = jnp.arange(NX, dtype=jnp.float32) / NX
    along = jnp.arange(NY, dtype=jnp.float32) / NY
    offsets = 0.3 * jnp.clip(jax.random.normal(second, (NZ,), jnp.float32), -1.0, 1.0)
    ramp = 0.5 + 0.5 * across[:, None, None] + 0.5 * along[None, :, None]
    noise = jnp.clip(jax.random.normal(first, (NX, NY, NZ), jnp.float32), -4.0, 4.0)
    return 1.0 + 0.01 * (ramp + offsets[None, None, :] + noise)


def set_ends(result, rng, smallest, largest):
    longest = result.shape.index(max(result.shape))
    spots = []
    for shift in (0, 1):
        where = [jax.random.randint(jax.random.fold_in(rng, axis), (), 0, length) for axis, length in enumerate(result.shape)]
        where[longest] = (where[longest] + shift) % result.shape[longest]
        spots.append(tuple(where))
    return result.at[spots[0]].set(smallest).at[spots[1]].set(largest)


def shard_levels(own_key, extent, shards, smallest, high):
    loudness = 1.0
    for axis_at, parts in shards:
        steps = jax.random.uniform(jax.random.fold_in(jax.random.fold_in(own_key, 6), axis_at), (parts,), jnp.float32, smallest / len(shards), high / len(shards))
        loudness = loudness * jnp.repeat(jnp.exp(steps), extent[axis_at] // parts).reshape((-1,) + (1,) * (len(extent) - 1 - axis_at))
    return loudness


def bell_draw(rng, dims, deviation, limit, shards=(), kind=jnp.bfloat16):
    entries = deviation * jax.random.normal(rng, dims, jnp.float32)
    if shards:
        entries = entries * shard_levels(rng, dims, shards, -0.22, 0.18)
    return jnp.clip(entries, -limit, limit).astype(kind)


def setup_inputs(seed: int = 0) -> dict:
    key_list = jax.random.split(jax.random.key(seed), 11)
    eastward = bell_draw(key_list[0], (NX, NY, NZ), 1.0, 6.0, ((0, 32), (1, 8)), jnp.float32)
    northward = bell_draw(key_list[1], (NX, NY, NZ), 1.0, 6.0, ((0, 32), (1, 8)), jnp.float32)
    vertical = bell_draw(key_list[2], (NX, NY, NZ), 1.0, 6.0, ((0, 32), (1, 8)), jnp.float32)
    pressure = bell_draw(key_list[3], (NX, NY, NZ), 1.0, 6.0, ((0, 32), (1, 8)), jnp.float32)
    theta = bell_draw(key_list[4], (NX, NY, NZ), 1.0, 6.0, ((0, 32), (1, 8)), jnp.float32)
    humidity = draw_humidity(jax.random.fold_in(key_list[10], 71), 0)
    sound_speed = jnp.clip(jnp.exp(jax.random.uniform(key_list[6], (NZ,), jnp.float32, math.log(0.25), math.log(1.0))), 0.25, 1.0)
    radius_sq = jnp.clip(0.25 + 3.75 * jax.random.uniform(key_list[7], (SLOTS, CLOUD, NX, NY), jnp.float32) ** shard_levels(key_list[7], (SLOTS, CLOUD, NX, NY), ((2, 32), (3, 8)), -0.2, 0.2), 0.25, 4.0)
    multiplicity = jnp.clip(jnp.exp(math.log(2.0) - 1.3862944 * jax.random.uniform(key_list[8], (SLOTS, CLOUD, NX, NY), jnp.float32) ** shard_levels(key_list[8], (SLOTS, CLOUD, NX, NY), ((2, 32), (3, 8)), -0.2, 0.2)), 0.5, 2.0).astype(jnp.bfloat16)
    droplet_count = set_ends(jax.random.randint(key_list[9], (CLOUD, NX, NY), 0, SLOTS + 1), jax.random.fold_in(key_list[9], 1), 0, SLOTS).astype(jnp.int32)
    return {"eastward": eastward, "northward": northward, "vertical": vertical, "pressure": pressure, "theta": theta, "humidity": humidity, "sound_speed": sound_speed, "radius_sq": radius_sq, "multiplicity": multiplicity, "droplet_count": droplet_count}


TIME_STEP = 1.0
BUOYANCY = 0.5
VAPOUR_SLOPE = 0.01
GROWTH_RATE = 25.0
RADIUS_FLOOR = 0.0625
MASS_FACTOR = 0.0004
LATENT_HEAT = 200.0

def column_matrix(sound_speed):
    levels = sound_speed.shape[0]
    rows = lax.broadcasted_iota(jnp.int32, (levels, levels), 0)
    cols = lax.broadcasted_iota(jnp.int32, (levels, levels), 1)
    inside = rows < levels - 1
    gradient = jnp.where(inside & (cols == rows + 1), 1.0, 0.0) - jnp.where(inside & (cols == rows), 1.0, 0.0)
    gradient = gradient.astype(jnp.float32)
    scaled = gradient * sound_speed[None, :]
    product = jnp.dot(scaled.astype(jnp.float32), gradient.T.astype(jnp.float32), precision=lax.Precision.HIGHEST, preferred_element_type=jnp.float32)
    return jnp.eye(levels, dtype=jnp.float32) + TIME_STEP * TIME_STEP * product

def column_update(pressure, vertical, heat, divergence, sound_speed, inverse):
    levels = pressure.shape[-1]
    interior = (lax.broadcasted_iota(jnp.int32, (levels,), 0) < levels - 1).astype(jnp.float32)
    explicit = pressure - TIME_STEP * sound_speed * divergence
    upward = jnp.concatenate([explicit[..., 1:] - explicit[..., :-1], jnp.zeros_like(explicit[..., :1])], axis=-1)
    source = interior * (vertical + TIME_STEP * BUOYANCY * heat) - TIME_STEP * upward
    flat = source.reshape(-1, levels)
    solved = jnp.dot(flat.astype(jnp.float32), inverse.astype(jnp.float32), precision=lax.Precision.HIGHEST, preferred_element_type=jnp.float32).reshape(source.shape)
    masked = solved * interior
    below = jnp.concatenate([jnp.zeros_like(masked[..., :1]), masked[..., :-1]], axis=-1)
    return (explicit - TIME_STEP * sound_speed * (masked - below), solved)

def reference(eastward, northward, vertical, pressure, theta, humidity, sound_speed, radius_sq, multiplicity, droplet_count):
    sat = humidity * jnp.exp(-VAPOUR_SLOPE * theta) - 1.0
    cloud = jnp.transpose(sat[:, :, CLOUD_BASE:CLOUD_BASE + CLOUD], (2, 0, 1))
    grown = jnp.maximum(radius_sq + GROWTH_RATE * cloud[None], RADIUS_FLOOR)
    live = lax.broadcasted_iota(jnp.int32, radius_sq.shape, 0) < droplet_count[None]
    mass = multiplicity.astype(jnp.float32) * (grown * jnp.sqrt(grown) - radius_sq * jnp.sqrt(radius_sq))
    change = MASS_FACTOR * lax.optimization_barrier(jnp.sum(jnp.where(live, mass, 0.0), axis=0))
    added = jnp.pad(jnp.transpose(change, (1, 2, 0)), ((0, 0), (0, 0), (CLOUD_BASE, NZ - CLOUD_BASE - CLOUD)))
    humidity_out = humidity - added
    theta_out = theta + LATENT_HEAT * added
    radius_out = jnp.where(live, grown, 0.0)
    percent = 100.0 * (humidity_out * jnp.exp(-VAPOUR_SLOPE * theta_out) - 1.0)
    saturation_profile = lax.optimization_barrier(jnp.mean(percent, axis=(0, 1)))
    theta_mean = lax.optimization_barrier(jnp.mean(theta_out, axis=(0, 1)))
    heat = theta_out - theta_mean
    inverse = jnp.linalg.inv(column_matrix(sound_speed))
    for substep in range(SUB):
        grad_east = (jnp.roll(pressure, -1, 0) - jnp.roll(pressure, 1, 0)) * 0.5
        grad_north = (jnp.roll(pressure, -1, 1) - jnp.roll(pressure, 1, 1)) * 0.5
        eastward = eastward - TIME_STEP * grad_east
        northward = northward - TIME_STEP * grad_north
        spread = (jnp.roll(eastward, -1, 0) - jnp.roll(eastward, 1, 0) + jnp.roll(northward, -1, 1) - jnp.roll(northward, 1, 1)) * 0.5
        pressure, vertical = column_update(pressure, vertical, heat, spread, sound_speed, inverse)
    return (eastward, northward, vertical, pressure, theta_out, humidity_out, radius_out, saturation_profile)
```

```python
import functools

import jax
import jax.numpy as jnp
from jax import lax
from jax.experimental import pallas as pl
from jax.experimental.pallas import tpu as pltpu
from jax.sharding import PartitionSpec as P

F32 = jnp.float32
BF16 = jnp.bfloat16
MESH = pl.DeviceIdType.MESH
X, Y, Z = 8, 128, 128
SLOTS, CLOUD, BASE = 64, 8, 32
ROWS = CLOUD * X
CHUNKS = 8
PER = SLOTS // CHUNKS
TOP = 8
SLOPE, GROWTH, FLOOR, MASS, LATENT, BUOYANCY = 0.01, 25.0, 0.0625, 0.0004, 200.0, 0.5


def split(x):
    high = x.astype(BF16)
    return high, (x - high.astype(F32)).astype(BF16)


def mm(a, b):
    return jnp.dot(a, b, preferred_element_type=F32)


def times(x, high, low):
    xh, xl = split(x)
    return mm(xh, high) + (mm(xl, high) + mm(xh, low))


def solve(forcing, explicit, high, low):
    both = times(jnp.concatenate([forcing, explicit], axis=1), high, low)
    return both[:, :Z], explicit + both[:, Z:]


def move_east(p, e_in, e_out, first, last):
    own = slice(TOP, TOP + Y)
    for a in range(first, last):
        e_out[a] = e_in[a] - 0.5 * (p[a + 2, own, :] - p[a, own, :])


def move_north(p, n_in, n_out, first, last):
    for i in range(X):
        n_out[i, first:last, :] = n_in[i, first:last, :] - 0.5 * (
            p[i + 2, first + 1 : last + 1, :] - p[i + 2, first - 1 : last - 1, :]
        )


def explicit_pressure(p, e, n, c, i):
    spread = 0.5 * (
        (e[i + 2] - e[i]) + (n[i, TOP + 1 : TOP + Y + 1, :] - n[i, TOP - 1 : TOP + Y - 1, :])
    )
    return p[i + 2, TOP : TOP + Y, :] - c * spread


def edges_north(p, n_in, n_out):
    move_north(p, n_in, n_out, TOP - 1, TOP)
    move_north(p, n_in, n_out, TOP, TOP + 8)
    move_north(p, n_in, n_out, TOP + Y - 8, TOP + Y)
    move_north(p, n_in, n_out, TOP + Y, TOP + Y + 1)


def column_matrix(c):
    k = lax.broadcasted_iota(jnp.int32, (Z, Z), 0)
    j = lax.broadcasted_iota(jnp.int32, (Z, Z), 1)
    here = jnp.broadcast_to(c, (Z, Z))
    above = pltpu.roll(here, Z - 1, 1)
    m = jnp.where(k == j, 1.0 + jnp.where(k < Z - 1, here + above, 0.0), 0.0)
    m = m - jnp.where((j == k + 1) & (j < Z - 1), here, 0.0)
    m = m - jnp.where((j == k - 1) & (k < Z - 1), above, 0.0)
    eye = jnp.where(k == j, 1.0, 0.0)
    return eye, eye - m * (1.0 / 3.0)


def column_tables(inverse, c):
    k = lax.broadcasted_iota(jnp.int32, (Z, Z), 0)
    a = jnp.where(k < Z - 1, inverse, 0.0)
    b = a - pltpu.roll(a, 1, 0)
    left = jnp.concatenate([a, b], axis=0)
    j = lax.broadcasted_iota(jnp.int32, (2 * Z, Z), 1)
    m = jnp.where(j < Z - 1, left, 0.0)
    right = (pltpu.roll(m, 1, 1) - m) * c
    return split(jnp.concatenate([left, right], axis=1))


def kernel_main(
    lo_size,
    e_hbm, n_hbm, v_hbm, p_hbm, th_hbm, hu_hbm, c_hbm, r_hbm, m_hbm, k_hbm,
    p2, e, n, f, th, hu, r, wh, wl, total,
    p0, p1, v, c_ref, m_ref, k_ref, cl, xr, r1, r2, r3,
    load_sem, r_sem, m_sem, hs, hr, as_, ar,
):
    gx, gy = lax.axis_index("gx"), lax.axis_index("gy")
    nx, ny = lax.axis_size("gx"), lax.axis_size("gy")
    hi_size = nx // lo_size
    lo, hi = lax.rem(gx, lo_size), gx // lo_size
    right, left = lax.rem(gx + 1, nx), lax.rem(gx + nx - 1, nx)
    up, down = lax.rem(gy + 1, ny), lax.rem(gy + ny - 1, ny)
    own = slice(TOP, TOP + Y)

    loads = []
    for at, (src, dst) in enumerate(
        (
            (th_hbm, th),
            (hu_hbm, hu),
            (k_hbm, k_ref),
            (c_hbm, c_ref),
            (p_hbm, p0.at[2:10, own, :]),
            (e_hbm, e.at[1:9]),
            (n_hbm, n.at[:, own, :]),
            (v_hbm, v),
        )
    ):
        loads.append(pltpu.make_async_copy(src, dst, load_sem.at[at]))

    def droplets(q):
        part = pl.ds(q * PER, PER)
        return (
            pltpu.make_async_copy(r_hbm.at[part], r.at[part], r_sem.at[q]),
            pltpu.make_async_copy(m_hbm.at[part], m_ref.at[part], m_sem.at[q]),
        )

    for copy in loads[:4]:
        copy.start()
    for q in range(CHUNKS):
        for copy in droplets(q):
            copy.start()
    for copy in loads[4:]:
        copy.start()

    barrier = pltpu.get_barrier_semaphore()
    peers = [(hi * lo_size + lax.rem(lo + d, lo_size), gy) for d in range(1, lo_size)]
    lo_peers = list(peers)
    hi_peers = [(lax.rem(hi + d, hi_size) * lo_size + lo, gy) for d in range(1, hi_size)]
    gy_peers = [(gx, lax.rem(gy + d, ny)) for d in range(1, ny)]
    everyone = [(left, gy), (right, gy)] + lo_peers + hi_peers + gy_peers
    for who in everyone:
        pl.semaphore_signal(barrier, inc=1, device_id=who, device_id_type=MESH)
    pl.semaphore_wait(barrier, len(everyone))

    def send(src, dst, at, who):
        return pltpu.make_async_remote_copy(
            src_ref=src,
            dst_ref=dst,
            send_sem=hs.at[at],
            recv_sem=hr.at[at],
            device_id=who,
            device_id_type=MESH,
        )

    def to_left(p, at):
        return send(p.at[2:4, own, :], p.at[10:12, own, :], at, (left, gy))

    def to_right(p, at):
        return send(p.at[8:10, own, :], p.at[0:2, own, :], at, (right, gy))

    def to_down(p, at):
        return send(p.at[2:10, TOP : TOP + 8, :], p.at[2:10, TOP + Y :, :], at, (gx, down))

    def to_up(p, at):
        return send(p.at[2:10, TOP + Y - 8 : TOP + Y, :], p.at[2:10, 0:TOP, :], at, (gx, up))

    halo0 = [
        send(p_hbm.at[0:2], p0.at[10:12, own, :], 0, (left, gy)),
        send(p_hbm.at[6:8], p0.at[0:2, own, :], 1, (right, gy)),
        send(e_hbm.at[0:1], e.at[9:10], 2, (left, gy)),
        send(e_hbm.at[7:8], e.at[0:1], 3, (right, gy)),
        send(p_hbm.at[:, 0:8, :], p0.at[2:10, TOP + Y :, :], 4, (gx, down)),
        send(p_hbm.at[:, Y - 8 :, :], p0.at[2:10, 0:TOP, :], 5, (gx, up)),
        send(n_hbm.at[:, 0:8, :], n.at[:, TOP + Y :, :], 6, (gx, down)),
        send(n_hbm.at[:, Y - 8 :, :], n.at[:, 0:TOP, :], 7, (gx, up)),
    ]
    for copy in halo0:
        copy.start()

    for copy in loads[:4]:
        copy.wait()
    c = c_ref[...]

    def saturation(i, _):
        sat = hu[i] * jnp.exp(-SLOPE * th[i]) - 1.0
        cl[:, pl.ds(i, 1), :] = GROWTH * jnp.transpose(sat)[BASE : BASE + CLOUD].reshape(CLOUD, 1, Y)
        return 0

    lax.fori_loop(0, X, saturation, 0)

    eye, r0 = column_matrix(c)
    xr[0:Z, :] = eye
    xr[Z:, :] = r0

    def condense(q, acc):
        for copy in droplets(q):
            copy.wait()
        growth = cl[...].reshape(ROWS, Y)
        count = k_ref[...].reshape(ROWS, Y)
        for s in range(PER):
            slot = q * PER + s
            old = r[slot]
            grown = jnp.maximum(old + growth, FLOOR)
            live = count > slot
            mass = m_ref[slot].astype(F32) * (
                grown * grown * lax.rsqrt(grown) - old * old * lax.rsqrt(old)
            )
            r[slot] = jnp.where(live, grown, 0.0)
            acc = acc + jnp.where(live, mass, 0.0)
        x = xr[...]
        high, low = split(x[Z:])
        product = times(x, high, low)
        xr[0:Z, :] = x[:Z] + product[:Z]
        xr[Z:, :] = product[Z:]
        return acc

    acc = lax.fori_loop(0, CHUNKS, condense, jnp.zeros((ROWS, Y), F32))
    cl[...] = (MASS * acc).reshape(CLOUD, X, Y)
    high, low = column_tables(xr[0:Z, :] * (1.0 / 3.0), c)
    wh[...] = high
    wl[...] = low

    def heating(i, sums):
        change = cl[:, pl.ds(i, 1), :].reshape(CLOUD, Y)
        added = jnp.transpose(
            jnp.concatenate(
                [jnp.zeros((BASE, Y), F32), change, jnp.zeros((Z - BASE - CLOUD, Y), F32)], axis=0
            )
        )
        wet = hu[i] - added
        warm = th[i] + LATENT * added
        hu[i] = wet
        th[i] = warm
        percent = 100.0 * (wet * jnp.exp(-SLOPE * warm) - 1.0)
        return (
            sums[0] + jnp.sum(percent.reshape(Y // 8, 8, Z), axis=0),
            sums[1] + jnp.sum(warm.reshape(Y // 8, 8, Z), axis=0),
        )

    zero = jnp.zeros((8, Z), F32)
    sums = lax.fori_loop(0, X, heating, (zero, zero))
    row = lax.broadcasted_iota(jnp.int32, (8, Z), 0)

    def gather(buffer, me, who, at):
        return [
            pltpu.make_async_remote_copy(
                src_ref=buffer.at[me],
                dst_ref=buffer.at[me],
                send_sem=as_.at[at + d],
                recv_sem=ar.at[at + d],
                device_id=peer,
                device_id_type=MESH,
            )
            for d, peer in enumerate(who)
        ]

    def add(buffer, count):
        value = buffer[0]
        for d in range(1, count):
            value = value + buffer[d]
        return value

    stage1 = gather(r1, lo, lo_peers, 0)
    stage2 = gather(r2, hi, hi_peers, len(lo_peers))
    stage3 = gather(r3, gy, gy_peers, len(lo_peers) + len(hi_peers))
    r1[lo] = jnp.where(
        row == 0,
        jnp.sum(sums[0], axis=0, keepdims=True),
        jnp.where(row == 1, jnp.sum(sums[1], axis=0, keepdims=True), 0.0),
    )
    for copy in stage1:
        copy.start()

    for copy in loads[4:]:
        copy.wait()

    def columns(p, i, count):
        forcing = jnp.concatenate([v[a] + BUOYANCY * th[a] for a in range(i, i + count)], axis=0)
        q = jnp.concatenate([explicit_pressure(p, e, n, c, a) for a in range(i, i + count)], axis=0)
        return forcing, q

    def step(p, p_next, i, last):
        vertical, pressure = solve(*columns(p, i, 2), wh[...], wl[...])
        for a in range(2):
            rows = slice(a * Y, (a + 1) * Y)
            p_next[i + a + 2, own, :] = pressure[rows]
            if last:
                f[i + a] = vertical[rows] + BUOYANCY * th[i + a]
            else:
                v[i + a] = vertical[rows]

    move_east(p0, e, e, 2, 8)
    move_north(p0, n, n, TOP + 8, TOP + Y - 8)
    for copy in halo0:
        copy.wait()
    move_east(p0, e, e, 0, 2)
    move_east(p0, e, e, 8, 10)
    edges_north(p0, n, n)
    halo1 = [to_left(p1, 8), to_right(p1, 9), to_down(p1, 10), to_up(p1, 11)]
    step(p0, p1, 0, False)
    halo1[0].start()
    step(p0, p1, 6, False)
    halo1[1].start()
    step(p0, p1, 2, False)
    step(p0, p1, 4, False)
    halo1[2].start()
    halo1[3].start()

    for copy in stage1:
        copy.wait()
    r2[hi] = add(r1, lo_size)
    for copy in stage2:
        copy.start()

    move_east(p1, e, e, 2, 8)
    move_north(p1, n, n, TOP + 8, TOP + Y - 8)
    for copy in halo1:
        copy.wait()
    move_east(p1, e, e, 0, 2)
    move_east(p1, e, e, 8, 10)
    edges_north(p1, n, n)
    halo2 = [to_left(p2, 12), to_right(p2, 13), to_down(p2, 14), to_up(p2, 15)]
    step(p1, p2, 0, True)
    halo2[0].start()
    step(p1, p2, 6, True)
    halo2[1].start()
    step(p1, p2, 2, True)
    step(p1, p2, 4, True)
    halo2[2].start()
    halo2[3].start()

    for copy in stage2:
        copy.wait()
    mean = add(r2, hi_size) * (1.0 / (nx * X * ny * Y))
    pull = jnp.broadcast_to(-BUOYANCY * mean[1:2, :], (8, Z))
    vertical, pressure = solve(pull, zero, wh[...], wl[...])
    vertical, pressure = solve(pull + vertical, pressure, wh[...], wl[...])
    vertical, pressure = solve(pull + vertical, pressure, wh[...], wl[...])
    r3[gy] = jnp.where(
        row == 0, mean, jnp.where(row == 1, vertical, jnp.where(row == 2, pressure, 0.0))
    )
    for copy in stage3:
        copy.start()
    for copy in halo2:
        copy.wait()
    for copy in stage3:
        copy.wait()
    total[...] = add(r3, ny)


def kernel_last(
    p, e, n, f, th, hu, r, wh, wl, total, c_ref,
    e_out, n_out, v_out, p_out, th_out, hu_out, r_out, s_out,
    e_new, n_new, v_new, p_new, sem,
):
    copies = []

    def out(src, dst):
        copy = pltpu.make_async_copy(src, dst, sem.at[len(copies)])
        copy.start()
        copies.append(copy)

    out(r, r_out)
    out(th, th_out)
    out(hu, hu_out)
    c = c_ref[...]
    stats = total[...]
    s_out[...] = stats[0:1, :]
    move_east(p, e, e_new, 0, 10)
    out(e_new.at[1:9], e_out)
    move_north(p, n, n_new, TOP + 8, TOP + Y - 8)
    edges_north(p, n, n_new)
    out(n_new.at[:, TOP : TOP + Y, :], n_out)
    for i in range(0, X, 2):
        forcing = jnp.concatenate([f[i], f[i + 1]], axis=0)
        q = jnp.concatenate(
            [explicit_pressure(p, e_new, n_new, c, a) for a in (i, i + 1)], axis=0
        )
        vertical, pressure = solve(forcing, q, wh[...], wl[...])
        vertical = vertical + stats[1:2, :]
        pressure = pressure + stats[2:3, :]
        for a in range(2):
            v_new[i + a] = vertical[a * Y : (a + 1) * Y]
            p_new[i + a] = pressure[a * Y : (a + 1) * Y]
        out(v_new.at[i : i + 2], v_out.at[i : i + 2])
        out(p_new.at[i : i + 2], p_out.at[i : i + 2])
    for copy in copies:
        copy.wait()


def local(lo_size, nx, ny, e, n, v, p, th, hu, sound_speed, radius, multiplicity, count):
    c = sound_speed.reshape(1, Z)
    radius = radius.reshape(SLOTS, ROWS, Y)
    multiplicity = multiplicity.reshape(SLOTS, ROWS, Y)
    stay = pltpu.with_memory_space_constraint
    hbm = pl.BlockSpec(memory_space=pltpu.HBM)
    vmem = pl.BlockSpec(memory_space=pltpu.VMEM)
    dma = pltpu.SemaphoreType.DMA
    hi_size = nx // lo_size
    peers = lo_size + hi_size + ny - 3
    handed = [
        ((X + 4, Y + 16, Z), F32),
        ((X + 2, Y, Z), F32),
        ((X, Y + 16, Z), F32),
        ((X, Y, Z), F32),
        ((X, Y, Z), F32),
        ((X, Y, Z), F32),
        ((SLOTS, ROWS, Y), F32),
        ((2 * Z, 2 * Z), BF16),
        ((2 * Z, 2 * Z), BF16),
        ((8, Z), F32),
    ]
    state = pl.pallas_call(
        functools.partial(kernel_main, lo_size),
        out_shape=tuple(pltpu.VMEM(s, d) for s, d in handed),
        in_specs=[hbm] * 10,
        out_specs=tuple([vmem] * len(handed)),
        scratch_shapes=[
            pltpu.VMEM((X + 4, Y + 16, Z), F32),
            pltpu.VMEM((X + 4, Y + 16, Z), F32),
            pltpu.VMEM((X, Y, Z), F32),
            pltpu.VMEM((1, Z), F32),
            pltpu.VMEM((SLOTS, ROWS, Y), BF16),
            pltpu.VMEM((CLOUD, X, Y), jnp.int32),
            pltpu.VMEM((CLOUD, X, Y), F32),
            pltpu.VMEM((2 * Z, Z), F32),
            pltpu.VMEM((lo_size, 8, Z), F32),
            pltpu.VMEM((hi_size, 8, Z), F32),
            pltpu.VMEM((ny, 8, Z), F32),
            dma((8,)),
            dma((CHUNKS,)),
            dma((CHUNKS,)),
            dma((16,)),
            dma((16,)),
            dma((peers,)),
            dma((peers,)),
        ],
        compiler_params=pltpu.CompilerParams(
            collective_id=0, has_side_effects=True, vmem_limit_bytes=24 << 20
        ),
        name="condense_and_step",
    )(*(stay(x, pltpu.HBM) for x in (e, n, v, p, th, hu, c, radius, multiplicity, count)))
    grid = jax.ShapeDtypeStruct((X, Y, Z), F32)
    outs = pl.pallas_call(
        kernel_last,
        out_shape=(
            (grid,) * 6
            + (
                jax.ShapeDtypeStruct((SLOTS, ROWS, Y), F32),
                jax.ShapeDtypeStruct((1, Z), F32),
            )
        ),
        in_specs=[vmem] * (len(handed) + 1),
        out_specs=tuple([hbm] * 7 + [vmem]),
        scratch_shapes=[
            pltpu.VMEM((X + 2, Y, Z), F32),
            pltpu.VMEM((X, Y + 16, Z), F32),
            pltpu.VMEM((X, Y, Z), F32),
            pltpu.VMEM((X, Y, Z), F32),
            dma((13,)),
        ],
        compiler_params=pltpu.CompilerParams(vmem_limit_bytes=24 << 20),
        name="last_step",
    )(*state, c)
    return outs[:6] + (outs[6].reshape(SLOTS, CLOUD, X, Y), outs[7].reshape(Z))


def solution(mesh):
    nx, ny = mesh.shape["gx"], mesh.shape["gy"]
    lo_size = 8 if nx % 8 == 0 else 2
    grid = P("gx", "gy", None)
    drops = P(None, None, "gx", "gy")
    return jax.shard_map(
        functools.partial(local, lo_size, nx, ny),
        mesh=mesh,
        in_specs=(grid,) * 6 + (P(), drops, drops, P(None, "gx", "gy")),
        out_specs=(grid,) * 6 + (drops, P()),
        check_vma=False,
    )
```

```python
import functools

import jax
import jax.numpy as jnp
from jax import lax
from jax.experimental import pallas as pl
from jax.experimental.pallas import tpu as pltpu
from jax.sharding import PartitionSpec as P

F32 = jnp.float32
BF16 = jnp.bfloat16
MESH = pl.DeviceIdType.MESH
X, Y, Z = 8, 128, 128
SLOTS, CLOUD, BASE = 64, 8, 32
ROWS = CLOUD * X
CHUNKS = 8
PER = SLOTS // CHUNKS
TOP = 8
SLOPE, GROWTH, FLOOR, MASS, LATENT, BUOYANCY = 0.01, 25.0, 0.0625, 0.0004, 200.0, 0.5


def split(x):
    high = x.astype(BF16)
    return high, (x - high.astype(F32)).astype(BF16)


def mm(a, b):
    return jnp.dot(a, b, preferred_element_type=F32)


def times(x, high, low):
    xh, xl = split(x)
    rows = x.shape[0]
    both = mm(jnp.concatenate([xh, xl], axis=0), high)
    return both[:rows] + (both[rows:] + mm(xh, low))


def solve(forcing, explicit, high, low):
    both = times(jnp.concatenate([forcing, explicit], axis=1), high, low)
    return both[:, :Z], explicit + both[:, Z:]


OWN = slice(TOP, TOP + Y)


def move_east(p, e_in, e_out, planes):
    for a in planes:
        e_out[a] = e_in[a] - 0.5 * (p[a + 2, OWN, :] - p[a, OWN, :])


def move_north(p, n, first, last):
    for i in range(X):
        n[i, first:last, :] = n[i, first:last, :] - 0.5 * (
            p[i + 2, first + 1 : last + 1, :] - p[i + 2, first - 1 : last - 1, :]
        )


def explicit_pressure(p, east, west, n, c, i):
    spread = 0.5 * (
        (east - west) + (n[i, TOP + 1 : TOP + Y + 1, :] - n[i, TOP - 1 : TOP + Y - 1, :])
    )
    return p[i + 2, OWN, :] - c * spread


def edges_north(p, n):
    move_north(p, n, TOP - 1, TOP)
    move_north(p, n, TOP, TOP + 8)
    move_north(p, n, TOP + Y - 8, TOP + Y)
    move_north(p, n, TOP + Y, TOP + Y + 1)


def column_matrix(c):
    k = lax.broadcasted_iota(jnp.int32, (Z, Z), 0)
    j = lax.broadcasted_iota(jnp.int32, (Z, Z), 1)
    here = jnp.broadcast_to(c, (Z, Z))
    above = pltpu.roll(here, Z - 1, 1)
    m = jnp.where(k == j, 1.0 + jnp.where(k < Z - 1, here + above, 0.0), 0.0)
    m = m - jnp.where((j == k + 1) & (j < Z - 1), here, 0.0)
    m = m - jnp.where((j == k - 1) & (k < Z - 1), above, 0.0)
    eye = jnp.where(k == j, 1.0, 0.0)
    return eye, eye - m * (1.0 / 3.0)


def column_tables(inverse, c):
    k = lax.broadcasted_iota(jnp.int32, (Z, Z), 0)
    a = jnp.where(k < Z - 1, inverse, 0.0)
    b = a - pltpu.roll(a, 1, 0)
    left = jnp.concatenate([a, b], axis=0)
    j = lax.broadcasted_iota(jnp.int32, (2 * Z, Z), 1)
    m = jnp.where(j < Z - 1, left, 0.0)
    right = (pltpu.roll(m, 1, 1) - m) * c
    return split(jnp.concatenate([left, right], axis=1))


def far_first(count):
    return sorted(range(1, count), key=lambda d: -min(d, count - d))


def kernel_main(
    lo_size,
    e_hbm, n_hbm, v_hbm, p_hbm, th_hbm, hu_hbm, c_hbm, r_hbm, m_hbm, k_hbm,
    p2, e, n, f, th, hu, r, wh, wl, v_new, p_new, total,
    p0, p1, v, c_ref, m_ref, k_ref, cl, xr, a_ref, r1, r2, r3,
    load_sem, r_sem, m_sem, hs, hr, as_, ar,
):
    gx, gy = lax.axis_index("gx"), lax.axis_index("gy")
    nx, ny = lax.axis_size("gx"), lax.axis_size("gy")
    hi_size = nx // lo_size
    lo, hi = lax.rem(gx, lo_size), gx // lo_size
    right, left = lax.rem(gx + 1, nx), lax.rem(gx + nx - 1, nx)
    up, down = lax.rem(gy + 1, ny), lax.rem(gy + ny - 1, ny)

    barrier = pltpu.get_barrier_semaphore()
    lo_peers = [(hi * lo_size + lax.rem(lo + d, lo_size), gy) for d in far_first(lo_size)]
    hi_peers = [(lax.rem(hi + d, hi_size) * lo_size + lo, gy) for d in far_first(hi_size)]
    gy_peers = [(gx, lax.rem(gy + d, ny)) for d in far_first(ny)]
    everyone = gy_peers + hi_peers + lo_peers + [(left, gy), (right, gy)]
    for who in everyone:
        pl.semaphore_signal(barrier, inc=1, device_id=who, device_id_type=MESH)

    def droplets(q):
        part = pl.ds(q * PER, PER)
        return (
            pltpu.make_async_copy(r_hbm.at[part], r.at[part], r_sem.at[q]),
            pltpu.make_async_copy(m_hbm.at[part], m_ref.at[part], m_sem.at[q]),
        )

    pairs = (
        (c_hbm, c_ref),
        (th_hbm, th),
        (hu_hbm, hu),
        (p_hbm.at[0:2], p0.at[2:4, OWN, :]),
        (p_hbm.at[6:8], p0.at[8:10, OWN, :]),
        (e_hbm.at[0:1], e.at[1:2]),
        (e_hbm.at[7:8], e.at[8:9]),
        (k_hbm, k_ref),
        (p_hbm.at[2:6], p0.at[4:8, OWN, :]),
        (e_hbm.at[1:7], e.at[2:8]),
        (n_hbm, n.at[:, OWN, :]),
        (v_hbm, v),
    )
    loads = [
        pltpu.make_async_copy(src, dst, load_sem.at[at]) for at, (src, dst) in enumerate(pairs)
    ]
    for copy in loads[:8]:
        copy.start()
    for q in range(CHUNKS):
        for copy in droplets(q):
            copy.start()
    for copy in loads[8:]:
        copy.start()

    loads[0].wait()
    c = c_ref[...]
    eye, r0 = column_matrix(c)
    xr[0:Z, :] = eye
    xr[Z:, :] = r0

    def square(_, carry):
        x = xr[...]
        high, low = split(x[Z:])
        product = times(x, high, low)
        xr[0:Z, :] = x[:Z] + product[:Z]
        xr[Z:, :] = product[Z:]
        return carry

    lax.fori_loop(0, 6, square, 0)
    high, low = column_tables(xr[0:Z, :] * (1.0 / 3.0), c)
    wh[...] = high
    wl[...] = low

    loads[1].wait()
    loads[2].wait()
    for i in range(X):
        sat = hu[i] * jnp.exp(-SLOPE * th[i]) - 1.0
        cl[:, i : i + 1, :] = GROWTH * jnp.transpose(sat)[BASE : BASE + CLOUD].reshape(CLOUD, 1, Y)

    for copy in loads[3:7]:
        copy.wait()
    a_ref[0] = e[1] - 0.5 * p0[3, OWN, :]
    a_ref[1] = e[8] + 0.5 * p0[8, OWN, :]

    pl.semaphore_wait(barrier, len(everyone))

    def send(src, dst, at, who):
        return pltpu.make_async_remote_copy(
            src_ref=src,
            dst_ref=dst,
            send_sem=hs.at[at],
            recv_sem=hr.at[at],
            device_id=who,
            device_id_type=MESH,
        )

    def exchange(p, at):
        return [
            send(p.at[2:3, OWN, :], p.at[10:11, OWN, :], at, (left, gy)),
            send(p.at[9:10, OWN, :], p.at[1:2, OWN, :], at + 1, (right, gy)),
            send(p.at[3:4, OWN, :], p.at[11:12, OWN, :], at + 2, (left, gy)),
            send(p.at[8:9, OWN, :], p.at[0:1, OWN, :], at + 3, (right, gy)),
            send(p.at[2:10, TOP : TOP + 8, :], p.at[2:10, TOP + Y :, :], at + 4, (gx, down)),
            send(p.at[2:10, TOP + Y - 8 : TOP + Y, :], p.at[2:10, 0:TOP, :], at + 5, (gx, up)),
        ]

    halo0 = [
        send(p_hbm.at[0:1], p0.at[10:11, OWN, :], 0, (left, gy)),
        send(p_hbm.at[7:8], p0.at[1:2, OWN, :], 1, (right, gy)),
        send(a_ref.at[0:1], e.at[9:10], 2, (left, gy)),
        send(a_ref.at[1:2], e.at[0:1], 3, (right, gy)),
        send(p_hbm.at[:, 0:8, :], p0.at[2:10, TOP + Y :, :], 4, (gx, down)),
        send(p_hbm.at[:, Y - 8 :, :], p0.at[2:10, 0:TOP, :], 5, (gx, up)),
        send(n_hbm.at[:, 0:8, :], n.at[:, TOP + Y :, :], 6, (gx, down)),
        send(n_hbm.at[:, Y - 8 :, :], n.at[:, 0:TOP, :], 7, (gx, up)),
    ]
    for copy in halo0:
        copy.start()
    halo1, halo2 = exchange(p1, 8), exchange(p2, 14)

    loads[7].wait()

    def condense(q, acc):
        for copy in droplets(q):
            copy.wait()
        growth = cl[...].reshape(ROWS, Y)
        count = k_ref[...].reshape(ROWS, Y)
        for s in range(PER):
            slot = q * PER + s
            old = r[slot]
            grown = jnp.maximum(old + growth, FLOOR)
            live = count > slot
            mass = m_ref[slot].astype(F32) * (
                grown * grown * lax.rsqrt(grown) - old * old * lax.rsqrt(old)
            )
            r[slot] = jnp.where(live, grown, 0.0)
            acc = acc + jnp.where(live, mass, 0.0)
        return acc

    acc = lax.fori_loop(0, CHUNKS, condense, jnp.zeros((ROWS, Y), F32))
    cl[...] = (MASS * acc).reshape(CLOUD, X, Y)

    zero = jnp.zeros((8, Z), F32)
    percents, warms = zero, zero
    for i in range(X):
        change = cl[:, i : i + 1, :].reshape(CLOUD, Y)
        added = jnp.transpose(
            jnp.concatenate(
                [jnp.zeros((BASE, Y), F32), change, jnp.zeros((Z - BASE - CLOUD, Y), F32)], axis=0
            )
        )
        wet = hu[i] - added
        warm = th[i] + LATENT * added
        hu[i] = wet
        th[i] = warm
        percent = 100.0 * (wet * jnp.exp(-SLOPE * warm) - 1.0)
        percents = percents + jnp.sum(percent.reshape(Y // 8, 8, Z), axis=0)
        warms = warms + jnp.sum(warm.reshape(Y // 8, 8, Z), axis=0)
    row = lax.broadcasted_iota(jnp.int32, (8, Z), 0)

    def gather(buffer, me, who, at):
        return [
            pltpu.make_async_remote_copy(
                src_ref=buffer.at[me],
                dst_ref=buffer.at[me],
                send_sem=as_.at[at + d],
                recv_sem=ar.at[at + d],
                device_id=peer,
                device_id_type=MESH,
            )
            for d, peer in enumerate(who)
        ]

    def add(buffer, count):
        value = buffer[0]
        for d in range(1, count):
            value = value + buffer[d]
        return value

    stage1 = gather(r1, lo, lo_peers, 0)
    stage2 = gather(r2, hi, hi_peers, len(lo_peers))
    stage3 = gather(r3, gy, gy_peers, len(lo_peers) + len(hi_peers))
    r1[lo] = jnp.where(
        row == 0,
        jnp.sum(percents, axis=0, keepdims=True),
        jnp.where(row == 1, jnp.sum(warms, axis=0, keepdims=True), 0.0),
    )
    for copy in stage1:
        copy.start()

    for copy in loads[8:]:
        copy.wait()

    def planes(p, p_next, which, last):
        forcing = jnp.concatenate([v[a] + BUOYANCY * th[a] for a in which], axis=0)
        q = jnp.concatenate(
            [explicit_pressure(p, e[a + 2], e[a], n, c, a) for a in which], axis=0
        )
        vertical, pressure = solve(forcing, q, wh[...], wl[...])
        for at, a in enumerate(which):
            rows = slice(at * Y, (at + 1) * Y)
            p_next[a + 2, OWN, :] = pressure[rows]
            if last:
                f[a] = vertical[rows] + BUOYANCY * th[a]
            else:
                v[a] = vertical[rows]

    def inside(p, halo):
        move_east(p, e, e, range(2, 8))
        move_north(p, n, TOP + 8, TOP + Y - 8)
        for copy in halo[4:]:
            copy.wait()
        edges_north(p, n)

    inside(p0, halo0)
    planes(p0, p1, (2, 3, 4, 5), False)
    for copy in halo0[:4]:
        copy.wait()
    move_east(p0, e, e, (1, 8))
    e[0] = e[0] - 0.5 * p0[2, OWN, :]
    e[9] = e[9] + 0.5 * p0[9, OWN, :]
    planes(p0, p1, (0, 7), False)
    halo1[0].start()
    halo1[1].start()
    planes(p0, p1, (1, 6), False)
    for copy in halo1[2:]:
        copy.start()

    for copy in stage1:
        copy.wait()
    r2[hi] = add(r1, lo_size)
    for copy in stage2:
        copy.start()

    inside(p1, halo1)
    planes(p1, p2, (2, 3, 4, 5), True)
    for copy in stage2:
        copy.wait()
    r3[gy] = add(r2, hi_size)
    for copy in stage3:
        copy.start()
    for copy in halo1[:4]:
        copy.wait()
    move_east(p1, e, e, (0, 1, 8, 9))
    planes(p1, p2, (0, 7), True)
    halo2[0].start()
    halo2[1].start()
    planes(p1, p2, (1, 6), True)
    for copy in halo2[2:]:
        copy.start()

    for copy in stage3:
        copy.wait()
    mean = add(r3, ny) * (1.0 / (nx * X * ny * Y))
    pull = jnp.broadcast_to(-BUOYANCY * mean[1:2, :], (16, Z))
    vertical, pressure = solve(pull, jnp.zeros((16, Z), F32), wh[...], wl[...])
    vertical, pressure = solve(pull + vertical, pressure, wh[...], wl[...])
    vertical, pressure = solve(pull + vertical, pressure, wh[...], wl[...])
    total[...] = jnp.where(row == 0, mean, jnp.where(row == 1, vertical[:8], pressure[:8]))

    inside(p2, halo2)
    which = (2, 3, 4, 5)
    forcing = jnp.concatenate([f[a] for a in which], axis=0)
    q = jnp.concatenate([explicit_pressure(p2, e[a + 2], e[a], n, c, a) for a in which], axis=0)
    inner_v, inner_p = solve(forcing, q, wh[...], wl[...])
    v_new[...] = (inner_v + vertical[0:1]).reshape(4, Y, Z)
    p_new[...] = (inner_p + pressure[0:1]).reshape(4, Y, Z)
    for copy in halo2[:4]:
        copy.wait()


def kernel_last(
    p, e, n, f, th, hu, r, wh, wl, v_in, p_in, total, c_ref,
    e_out, n_out, v_out, p_out, th_out, hu_out, r_out, s_out,
    e_new, v_new, p_new, sem,
):
    copies = []

    def out(src, dst):
        copy = pltpu.make_async_copy(src, dst, sem.at[len(copies)])
        copy.start()
        copies.append(copy)

    out(r, r_out)
    out(th, th_out)
    out(hu, hu_out)
    out(n.at[:, OWN, :], n_out)
    out(e.at[2:8], e_out.at[1:7])
    out(v_in, v_out.at[2:6])
    out(p_in, p_out.at[2:6])
    c = c_ref[...]
    stats = total[...]
    s_out[...] = stats[0:1, :]
    for at, a in enumerate((0, 1, 8, 9)):
        e_new[at] = e[a] - 0.5 * (p[a + 2, OWN, :] - p[a, OWN, :])
    out(e_new.at[1:2], e_out.at[0:1])
    out(e_new.at[2:3], e_out.at[7:8])
    forcing = jnp.concatenate([f[0], f[1], f[6], f[7]], axis=0)
    q = jnp.concatenate(
        [
            explicit_pressure(p, e[2], e_new[0], n, c, 0),
            explicit_pressure(p, e[3], e_new[1], n, c, 1),
            explicit_pressure(p, e_new[2], e[6], n, c, 6),
            explicit_pressure(p, e_new[3], e[7], n, c, 7),
        ],
        axis=0,
    )
    vertical, pressure = solve(forcing, q, wh[...], wl[...])
    v_new[...] = (vertical + stats[1:2, :]).reshape(4, Y, Z)
    p_new[...] = (pressure + stats[2:3, :]).reshape(4, Y, Z)
    out(v_new.at[0:2], v_out.at[0:2])
    out(p_new.at[0:2], p_out.at[0:2])
    out(v_new.at[2:4], v_out.at[6:8])
    out(p_new.at[2:4], p_out.at[6:8])
    for copy in copies:
        copy.wait()


def local(lo_size, nx, ny, e, n, v, p, th, hu, sound_speed, radius, multiplicity, count):
    c = sound_speed.reshape(1, Z)
    radius = radius.reshape(SLOTS, ROWS, Y)
    multiplicity = multiplicity.reshape(SLOTS, ROWS, Y)
    stay = pltpu.with_memory_space_constraint
    hbm = pl.BlockSpec(memory_space=pltpu.HBM)
    vmem = pl.BlockSpec(memory_space=pltpu.VMEM)
    dma = pltpu.SemaphoreType.DMA
    hi_size = nx // lo_size
    peers = lo_size + hi_size + ny - 3
    handed = [
        ((X + 4, Y + 16, Z), F32),
        ((X + 2, Y, Z), F32),
        ((X, Y + 16, Z), F32),
        ((X, Y, Z), F32),
        ((X, Y, Z), F32),
        ((X, Y, Z), F32),
        ((SLOTS, ROWS, Y), F32),
        ((2 * Z, 2 * Z), BF16),
        ((2 * Z, 2 * Z), BF16),
        ((4, Y, Z), F32),
        ((4, Y, Z), F32),
        ((8, Z), F32),
    ]
    state = pl.pallas_call(
        functools.partial(kernel_main, lo_size),
        out_shape=tuple(pltpu.VMEM(s, d) for s, d in handed),
        in_specs=[hbm] * 10,
        out_specs=tuple([vmem] * len(handed)),
        scratch_shapes=[
            pltpu.VMEM((X + 4, Y + 16, Z), F32),
            pltpu.VMEM((X + 4, Y + 16, Z), F32),
            pltpu.VMEM((X, Y, Z), F32),
            pltpu.VMEM((1, Z), F32),
            pltpu.VMEM((SLOTS, ROWS, Y), BF16),
            pltpu.VMEM((CLOUD, X, Y), jnp.int32),
            pltpu.VMEM((CLOUD, X, Y), F32),
            pltpu.VMEM((2 * Z, Z), F32),
            pltpu.VMEM((2, Y, Z), F32),
            pltpu.VMEM((lo_size, 8, Z), F32),
            pltpu.VMEM((hi_size, 8, Z), F32),
            pltpu.VMEM((ny, 8, Z), F32),
            dma((12,)),
            dma((CHUNKS,)),
            dma((CHUNKS,)),
            dma((20,)),
            dma((20,)),
            dma((peers,)),
            dma((peers,)),
        ],
        compiler_params=pltpu.CompilerParams(
            collective_id=0, has_side_effects=True, vmem_limit_bytes=24 << 20
        ),
        name="condense_and_step",
    )(*(stay(x, pltpu.HBM) for x in (e, n, v, p, th, hu, c, radius, multiplicity, count)))
    grid = jax.ShapeDtypeStruct((X, Y, Z), F32)
    outs = pl.pallas_call(
        kernel_last,
        out_shape=(
            (grid,) * 6
            + (
                jax.ShapeDtypeStruct((SLOTS, ROWS, Y), F32),
                jax.ShapeDtypeStruct((1, Z), F32),
            )
        ),
        in_specs=[vmem] * (len(handed) + 1),
        out_specs=tuple([hbm] * 7 + [vmem]),
        scratch_shapes=[
            pltpu.VMEM((4, Y, Z), F32),
            pltpu.VMEM((4, Y, Z), F32),
            pltpu.VMEM((4, Y, Z), F32),
            dma((13,)),
        ],
        compiler_params=pltpu.CompilerParams(vmem_limit_bytes=24 << 20),
        name="last_step",
    )(*state, c)
    return outs[:6] + (outs[6].reshape(SLOTS, CLOUD, X, Y), outs[7].reshape(Z))


def solution(mesh):
    nx, ny = mesh.shape["gx"], mesh.shape["gy"]
    lo_size = 8 if nx % 8 == 0 else 2
    grid = P("gx", "gy", None)
    drops = P(None, None, "gx", "gy")
    return jax.shard_map(
        functools.partial(local, lo_size, nx, ny),
        mesh=mesh,
        in_specs=(grid,) * 6 + (P(), drops, drops, P(None, "gx", "gy")),
        out_specs=(grid,) * 6 + (drops, P()),
        check_vma=False,
    )
```

```python
import functools

import jax
import jax.numpy as jnp
from jax import lax
from jax.experimental import pallas as pl
from jax.experimental.pallas import tpu as pltpu
from jax.sharding import PartitionSpec as P

F32 = jnp.float32
BF16 = jnp.bfloat16
MESH = pl.DeviceIdType.MESH
X, Y, Z = 8, 128, 128
SLOTS, CLOUD, BASE = 64, 8, 32
ROWS = CLOUD * X
CHUNKS = 8
PER = SLOTS // CHUNKS
TOP = 8
SLOPE, GROWTH, FLOOR, MASS, LATENT, BUOYANCY = 0.01, 25.0, 0.0625, 0.0004, 200.0, 0.5


def split(x):
    high = x.astype(BF16)
    return high, (x - high.astype(F32)).astype(BF16)


def mm(a, b):
    return jnp.dot(a, b, preferred_element_type=F32)


def times(x, high, low):
    xh, xl = split(x)
    rows = x.shape[0]
    both = mm(jnp.concatenate([xh, xl], axis=0), high)
    return both[:rows] + (both[rows:] + mm(xh, low))


def solve(forcing, explicit, high, low):
    both = times(jnp.concatenate([forcing, explicit], axis=1), high, low)
    return both[:, :Z], explicit + both[:, Z:]


OWN = slice(TOP, TOP + Y)


def move_east(p, e_in, e_out, planes):
    for a in planes:
        e_out[a] = e_in[a] - 0.5 * (p[a + 2, OWN, :] - p[a, OWN, :])


def move_north(p, n, first, last):
    for i in range(X):
        n[i, first:last, :] = n[i, first:last, :] - 0.5 * (
            p[i + 2, first + 1 : last + 1, :] - p[i + 2, first - 1 : last - 1, :]
        )


def explicit_pressure(p, east, west, n, c, i):
    spread = 0.5 * (
        (east - west) + (n[i, TOP + 1 : TOP + Y + 1, :] - n[i, TOP - 1 : TOP + Y - 1, :])
    )
    return p[i + 2, OWN, :] - c * spread


def edges_north(p, n):
    move_north(p, n, TOP - 1, TOP)
    move_north(p, n, TOP, TOP + 8)
    move_north(p, n, TOP + Y - 8, TOP + Y)
    move_north(p, n, TOP + Y, TOP + Y + 1)


def column_matrix(c):
    k = lax.broadcasted_iota(jnp.int32, (Z, Z), 0)
    j = lax.broadcasted_iota(jnp.int32, (Z, Z), 1)
    here = jnp.broadcast_to(c, (Z, Z))
    above = pltpu.roll(here, Z - 1, 1)
    m = jnp.where(k == j, 1.0 + jnp.where(k < Z - 1, here + above, 0.0), 0.0)
    m = m - jnp.where((j == k + 1) & (j < Z - 1), here, 0.0)
    m = m - jnp.where((j == k - 1) & (k < Z - 1), above, 0.0)
    eye = jnp.where(k == j, 1.0, 0.0)
    return eye, eye - m * (1.0 / 3.0)


def column_tables(inverse, c):
    k = lax.broadcasted_iota(jnp.int32, (Z, Z), 0)
    a = jnp.where(k < Z - 1, inverse, 0.0)
    b = a - pltpu.roll(a, 1, 0)
    left = jnp.concatenate([a, b], axis=0)
    j = lax.broadcasted_iota(jnp.int32, (2 * Z, Z), 1)
    m = jnp.where(j < Z - 1, left, 0.0)
    right = (pltpu.roll(m, 1, 1) - m) * c
    return split(jnp.concatenate([left, right], axis=1))


def far_first(count):
    return sorted(range(1, count), key=lambda d: -min(d, count - d))


def row_order(nh, ny):
    steps = [(h, y, c) for h in range(nh) for y in range(ny) for c in range(2)][1:]
    return sorted(steps, key=lambda t: -(min(t[0], nh - t[0]) + min(t[1], ny - t[1])) * 2 - t[2])


def kernel_main(
    lo_size,
    e_hbm, n_hbm, v_hbm, p_hbm, th_hbm, hu_hbm, c_hbm, r_hbm, m_hbm, k_hbm,
    p2, e, n, f, th, hu, r, wh, wl, v_new, p_new, total,
    p0, p1, v, c_ref, m_ref, k_ref, cl, xr, a_ref, r1, r3,
    load_sem, r_sem, m_sem, hs, hr, as_, ar, x_sem, z_sem,
):
    gx, gy = lax.axis_index("gx"), lax.axis_index("gy")
    nx, ny = lax.axis_size("gx"), lax.axis_size("gy")
    hi_size = nx // lo_size
    lo, hi = lax.rem(gx, lo_size), gx // lo_size
    right, left = lax.rem(gx + 1, nx), lax.rem(gx + nx - 1, nx)
    up, down = lax.rem(gy + 1, ny), lax.rem(gy + ny - 1, ny)

    barrier = pltpu.get_barrier_semaphore()
    lo_peers = [(hi * lo_size + lax.rem(lo + d, lo_size), gy) for d in range(1, lo_size)]
    hi_peers = [(lax.rem(hi + d, hi_size) * lo_size + lo, gy) for d in range(1, hi_size)]
    gy_peers = [(gx, lax.rem(gy + d, ny)) for d in far_first(ny)]
    relay = ny == 8
    gy_near = [(gx, lax.rem(gy + d, ny)) for d in (1, 2, 6, 7)] if relay else gy_peers
    gy_two = [(gx, lax.rem(gy + d, ny)) for d in (2, 6)] if relay else []
    everyone = gy_near + hi_peers + lo_peers + [(left, gy), (right, gy)]
    for who in everyone:
        pl.semaphore_signal(barrier, inc=1, device_id=who, device_id_type=MESH)
    row_peers = [
        (
            lax.rem(hi + dh, hi_size) * lo_size
            + lax.rem(lo // 2 + dy, lo_size // 2) * 2
            + lax.rem(lo + dc, 2),
            gy,
        )
        for dh, dy, dc in row_order(hi_size, lo_size // 2)
    ]

    def droplets(q):
        part = pl.ds(q * PER, PER)
        return (
            pltpu.make_async_copy(r_hbm.at[part], r.at[part], r_sem.at[q]),
            pltpu.make_async_copy(m_hbm.at[part], m_ref.at[part], m_sem.at[q]),
        )

    pairs = (
        (c_hbm, c_ref),
        (th_hbm, th),
        (hu_hbm, hu),
        (p_hbm.at[0:2], p0.at[2:4, OWN, :]),
        (p_hbm.at[6:8], p0.at[8:10, OWN, :]),
        (e_hbm.at[0:1], e.at[1:2]),
        (e_hbm.at[7:8], e.at[8:9]),
        (k_hbm, k_ref),
        (p_hbm.at[2:6], p0.at[4:8, OWN, :]),
        (e_hbm.at[1:7], e.at[2:8]),
        (n_hbm, n.at[:, OWN, :]),
        (v_hbm, v),
    )
    loads = [
        pltpu.make_async_copy(src, dst, load_sem.at[at]) for at, (src, dst) in enumerate(pairs)
    ]
    for copy in loads[:8]:
        copy.start()
    for q in range(CHUNKS):
        for copy in droplets(q):
            copy.start()
    for copy in loads[8:]:
        copy.start()

    loads[0].wait()
    c = c_ref[...]
    eye, r0 = column_matrix(c)
    xr[0:Z, :] = eye
    xr[Z:, :] = r0

    def square(_, carry):
        x = xr[...]
        high, low = split(x[Z:])
        product = times(x, high, low)
        xr[0:Z, :] = x[:Z] + product[:Z]
        xr[Z:, :] = product[Z:]
        return carry

    lax.fori_loop(0, 6, square, 0)
    high, low = column_tables(xr[0:Z, :] * (1.0 / 3.0), c)
    wh[...] = high
    wl[...] = low

    loads[1].wait()
    loads[2].wait()
    for i in range(X):
        sat = hu[i] * jnp.exp(-SLOPE * th[i]) - 1.0
        cl[:, i : i + 1, :] = GROWTH * jnp.transpose(sat)[BASE : BASE + CLOUD].reshape(CLOUD, 1, Y)

    for copy in loads[3:7]:
        copy.wait()
    a_ref[0] = e[1] - 0.5 * p0[3, OWN, :]
    a_ref[1] = e[8] + 0.5 * p0[8, OWN, :]

    pl.semaphore_wait(barrier, len(everyone))

    def send(src, dst, at, who):
        return pltpu.make_async_remote_copy(
            src_ref=src,
            dst_ref=dst,
            send_sem=hs.at[at],
            recv_sem=hr.at[at],
            device_id=who,
            device_id_type=MESH,
        )

    def exchange(p, at):
        return [
            send(p.at[2:3, OWN, :], p.at[10:11, OWN, :], at, (left, gy)),
            send(p.at[9:10, OWN, :], p.at[1:2, OWN, :], at + 1, (right, gy)),
            send(p.at[3:4, OWN, :], p.at[11:12, OWN, :], at + 2, (left, gy)),
            send(p.at[8:9, OWN, :], p.at[0:1, OWN, :], at + 3, (right, gy)),
            send(p.at[2:10, TOP : TOP + 8, :], p.at[2:10, TOP + Y :, :], at + 4, (gx, down)),
            send(p.at[2:10, TOP + Y - 8 : TOP + Y, :], p.at[2:10, 0:TOP, :], at + 5, (gx, up)),
        ]

    halo0 = [
        send(p_hbm.at[0:1], p0.at[10:11, OWN, :], 0, (left, gy)),
        send(p_hbm.at[7:8], p0.at[1:2, OWN, :], 1, (right, gy)),
        send(a_ref.at[0:1], e.at[9:10], 2, (left, gy)),
        send(a_ref.at[1:2], e.at[0:1], 3, (right, gy)),
        send(p_hbm.at[:, 0:8, :], p0.at[2:10, TOP + Y :, :], 4, (gx, down)),
        send(p_hbm.at[:, Y - 8 :, :], p0.at[2:10, 0:TOP, :], 5, (gx, up)),
        send(n_hbm.at[:, 0:8, :], n.at[:, TOP + Y :, :], 6, (gx, down)),
        send(n_hbm.at[:, Y - 8 :, :], n.at[:, 0:TOP, :], 7, (gx, up)),
    ]
    for copy in halo0:
        copy.start()
    for who in hi_peers:
        pl.semaphore_signal(x_sem, inc=1, device_id=who, device_id_type=MESH)
    for who in gy_two:
        pl.semaphore_signal(z_sem, inc=1, device_id=who, device_id_type=MESH)
    halo1, halo2 = exchange(p1, 8), exchange(p2, 14)

    loads[7].wait()

    def condense(q, acc):
        for copy in droplets(q):
            copy.wait()
        growth = cl[...].reshape(ROWS, Y)
        count = k_ref[...].reshape(ROWS, Y)
        for s in range(PER):
            slot = q * PER + s
            old = r[slot]
            grown = jnp.maximum(old + growth, FLOOR)
            live = count > slot
            mass = m_ref[slot].astype(F32) * (
                grown * grown * lax.rsqrt(grown) - old * old * lax.rsqrt(old)
            )
            r[slot] = jnp.where(live, grown, 0.0)
            acc = acc + jnp.where(live, mass, 0.0)
        return acc

    acc = lax.fori_loop(0, CHUNKS, condense, jnp.zeros((ROWS, Y), F32))
    cl[...] = (MASS * acc).reshape(CLOUD, X, Y)

    zero = jnp.zeros((8, Z), F32)
    percents, warms = zero, zero
    for i in range(X):
        change = cl[:, i : i + 1, :].reshape(CLOUD, Y)
        added = jnp.transpose(
            jnp.concatenate(
                [jnp.zeros((BASE, Y), F32), change, jnp.zeros((Z - BASE - CLOUD, Y), F32)], axis=0
            )
        )
        wet = hu[i] - added
        warm = th[i] + LATENT * added
        hu[i] = wet
        th[i] = warm
        percent = 100.0 * (wet * jnp.exp(-SLOPE * warm) - 1.0)
        percents = percents + jnp.sum(percent.reshape(Y // 8, 8, Z), axis=0)
        warms = warms + jnp.sum(warm.reshape(Y // 8, 8, Z), axis=0)
    row = lax.broadcasted_iota(jnp.int32, (8, Z), 0)

    def gather(buffer, me, who, at):
        return [
            pltpu.make_async_remote_copy(
                src_ref=buffer.at[me],
                dst_ref=buffer.at[me],
                send_sem=as_.at[at + d],
                recv_sem=ar.at[at + d],
                device_id=peer,
                device_id_type=MESH,
            )
            for d, peer in enumerate(who)
        ]

    def add(buffer, count):
        value = buffer[0]
        for d in range(1, count):
            value = value + buffer[d]
        return value

    stage1 = gather(r1, gx, row_peers, 0)
    stage2 = gather(r3, gy, gy_peers, len(row_peers))
    r1[gx] = jnp.where(
        row == 0,
        jnp.sum(percents, axis=0, keepdims=True),
        jnp.where(row == 1, jnp.sum(warms, axis=0, keepdims=True), 0.0),
    )
    pl.semaphore_wait(x_sem, len(hi_peers))
    for copy in stage1:
        copy.start()

    for copy in loads[8:]:
        copy.wait()

    def planes(p, p_next, which, last):
        forcing = jnp.concatenate([v[a] + BUOYANCY * th[a] for a in which], axis=0)
        q = jnp.concatenate(
            [explicit_pressure(p, e[a + 2], e[a], n, c, a) for a in which], axis=0
        )
        vertical, pressure = solve(forcing, q, wh[...], wl[...])
        for at, a in enumerate(which):
            rows = slice(at * Y, (at + 1) * Y)
            p_next[a + 2, OWN, :] = pressure[rows]
            if last:
                f[a] = vertical[rows] + BUOYANCY * th[a]
            else:
                v[a] = vertical[rows]

    def inside(p):
        move_east(p, e, e, range(2, 8))
        move_north(p, n, TOP + 8, TOP + Y - 8)

    def north_edges(p, halo):
        for copy in halo[4:]:
            copy.wait()
        edges_north(p, n)

    inside(p0)
    north_edges(p0, halo0)
    planes(p0, p1, (2, 3, 4, 5), False)
    for copy in halo0[:4]:
        copy.wait()
    move_east(p0, e, e, (1, 8))
    e[0] = e[0] - 0.5 * p0[2, OWN, :]
    e[9] = e[9] + 0.5 * p0[9, OWN, :]
    planes(p0, p1, (0, 7), False)
    halo1[0].start()
    halo1[1].start()
    planes(p0, p1, (1, 6), False)
    for copy in halo1[2:]:
        copy.start()

    inside(p1)
    for copy in stage1:
        copy.wait()
    r3[gy] = add(r1, nx)
    if relay:
        pl.semaphore_wait(z_sem, len(gy_two))
    for copy in stage2:
        copy.start()
    north_edges(p1, halo1)
    planes(p1, p2, (2, 3, 4, 5), True)
    for copy in halo1[:4]:
        copy.wait()
    move_east(p1, e, e, (0, 1, 8, 9))
    planes(p1, p2, (0, 7), True)
    halo2[0].start()
    halo2[1].start()
    planes(p1, p2, (1, 6), True)
    for copy in halo2[2:]:
        copy.start()

    inside(p2)
    for copy in stage2:
        copy.wait()
    mean = add(r3, ny) * (1.0 / (nx * X * ny * Y))
    pull = jnp.broadcast_to(-BUOYANCY * mean[1:2, :], (16, Z))
    vertical, pressure = solve(pull, jnp.zeros((16, Z), F32), wh[...], wl[...])
    vertical, pressure = solve(pull + vertical, pressure, wh[...], wl[...])
    vertical, pressure = solve(pull + vertical, pressure, wh[...], wl[...])
    total[...] = jnp.where(row == 0, mean, jnp.where(row == 1, vertical[:8], pressure[:8]))

    north_edges(p2, halo2)
    which = (2, 3, 4, 5)
    forcing = jnp.concatenate([f[a] for a in which], axis=0)
    q = jnp.concatenate([explicit_pressure(p2, e[a + 2], e[a], n, c, a) for a in which], axis=0)
    inner_v, inner_p = solve(forcing, q, wh[...], wl[...])
    v_new[...] = (inner_v + vertical[0:1]).reshape(4, Y, Z)
    p_new[...] = (inner_p + pressure[0:1]).reshape(4, Y, Z)
    for copy in halo2[:4]:
        copy.wait()


def kernel_last(
    p, e, n, f, th, hu, r, wh, wl, v_in, p_in, total, c_ref,
    e_out, n_out, v_out, p_out, th_out, hu_out, r_out, s_out,
    e_new, v_new, p_new, sem,
):
    copies = []

    def out(src, dst):
        copy = pltpu.make_async_copy(src, dst, sem.at[len(copies)])
        copy.start()
        copies.append(copy)

    out(r, r_out)
    out(th, th_out)
    out(hu, hu_out)
    out(n.at[:, OWN, :], n_out)
    out(e.at[2:8], e_out.at[1:7])
    out(v_in, v_out.at[2:6])
    out(p_in, p_out.at[2:6])
    c = c_ref[...]
    stats = total[...]
    s_out[...] = stats[0:1, :]
    for at, a in enumerate((0, 1, 8, 9)):
        e_new[at] = e[a] - 0.5 * (p[a + 2, OWN, :] - p[a, OWN, :])
    out(e_new.at[1:2], e_out.at[0:1])
    out(e_new.at[2:3], e_out.at[7:8])
    forcing = jnp.concatenate([f[0], f[1], f[6], f[7]], axis=0)
    q = jnp.concatenate(
        [
            explicit_pressure(p, e[2], e_new[0], n, c, 0),
            explicit_pressure(p, e[3], e_new[1], n, c, 1),
            explicit_pressure(p, e_new[2], e[6], n, c, 6),
            explicit_pressure(p, e_new[3], e[7], n, c, 7),
        ],
        axis=0,
    )
    vertical, pressure = solve(forcing, q, wh[...], wl[...])
    v_new[...] = (vertical + stats[1:2, :]).reshape(4, Y, Z)
    p_new[...] = (pressure + stats[2:3, :]).reshape(4, Y, Z)
    out(v_new.at[0:2], v_out.at[0:2])
    out(p_new.at[0:2], p_out.at[0:2])
    out(v_new.at[2:4], v_out.at[6:8])
    out(p_new.at[2:4], p_out.at[6:8])
    for copy in copies:
        copy.wait()


def local(lo_size, nx, ny, e, n, v, p, th, hu, sound_speed, radius, multiplicity, count):
    c = sound_speed.reshape(1, Z)
    radius = radius.reshape(SLOTS, ROWS, Y)
    multiplicity = multiplicity.reshape(SLOTS, ROWS, Y)
    stay = pltpu.with_memory_space_constraint
    hbm = pl.BlockSpec(memory_space=pltpu.HBM)
    vmem = pl.BlockSpec(memory_space=pltpu.VMEM)
    dma = pltpu.SemaphoreType.DMA
    peers = nx + ny - 2
    handed = [
        ((X + 4, Y + 16, Z), F32),
        ((X + 2, Y, Z), F32),
        ((X, Y + 16, Z), F32),
        ((X, Y, Z), F32),
        ((X, Y, Z), F32),
        ((X, Y, Z), F32),
        ((SLOTS, ROWS, Y), F32),
        ((2 * Z, 2 * Z), BF16),
        ((2 * Z, 2 * Z), BF16),
        ((4, Y, Z), F32),
        ((4, Y, Z), F32),
        ((8, Z), F32),
    ]
    state = pl.pallas_call(
        functools.partial(kernel_main, lo_size),
        out_shape=tuple(pltpu.VMEM(s, d) for s, d in handed),
        in_specs=[hbm] * 10,
        out_specs=tuple([vmem] * len(handed)),
        scratch_shapes=[
            pltpu.VMEM((X + 4, Y + 16, Z), F32),
            pltpu.VMEM((X + 4, Y + 16, Z), F32),
            pltpu.VMEM((X, Y, Z), F32),
            pltpu.VMEM((1, Z), F32),
            pltpu.VMEM((SLOTS, ROWS, Y), BF16),
            pltpu.VMEM((CLOUD, X, Y), jnp.int32),
            pltpu.VMEM((CLOUD, X, Y), F32),
            pltpu.VMEM((2 * Z, Z), F32),
            pltpu.VMEM((2, Y, Z), F32),
            pltpu.VMEM((nx, 8, Z), F32),
            pltpu.VMEM((ny, 8, Z), F32),
            dma((12,)),
            dma((CHUNKS,)),
            dma((CHUNKS,)),
            dma((20,)),
            dma((20,)),
            dma((peers,)),
            dma((peers,)),
            pltpu.SemaphoreType.REGULAR,
            pltpu.SemaphoreType.REGULAR,
        ],
        compiler_params=pltpu.CompilerParams(
            collective_id=0, has_side_effects=True, vmem_limit_bytes=24 << 20
        ),
        name="condense_and_step",
    )(*(stay(x, pltpu.HBM) for x in (e, n, v, p, th, hu, c, radius, multiplicity, count)))
    grid = jax.ShapeDtypeStruct((X, Y, Z), F32)
    outs = pl.pallas_call(
        kernel_last,
        out_shape=(
            (grid,) * 6
            + (
                jax.ShapeDtypeStruct((SLOTS, ROWS, Y), F32),
                jax.ShapeDtypeStruct((1, Z), F32),
            )
        ),
        in_specs=[vmem] * (len(handed) + 1),
        out_specs=tuple([hbm] * 7 + [vmem]),
        scratch_shapes=[
            pltpu.VMEM((4, Y, Z), F32),
            pltpu.VMEM((4, Y, Z), F32),
            pltpu.VMEM((4, Y, Z), F32),
            dma((13,)),
        ],
        compiler_params=pltpu.CompilerParams(vmem_limit_bytes=24 << 20),
        name="last_step",
    )(*state, c)
    return outs[:6] + (outs[6].reshape(SLOTS, CLOUD, X, Y), outs[7].reshape(Z))


def solution(mesh):
    nx, ny = mesh.shape["gx"], mesh.shape["gy"]
    lo_size = 8 if nx % 8 == 0 else 2
    grid = P("gx", "gy", None)
    drops = P(None, None, "gx", "gy")
    return jax.shard_map(
        functools.partial(local, lo_size, nx, ny),
        mesh=mesh,
        in_specs=(grid,) * 6 + (P(), drops, drops, P(None, "gx", "gy")),
        out_specs=(grid,) * 6 + (drops, P()),
        check_vma=False,
    )
```

```python
import functools

import jax
import jax.numpy as jnp
from jax import lax
from jax.experimental import pallas as pl
from jax.experimental.pallas import tpu as pltpu
from jax.sharding import PartitionSpec as P

F32 = jnp.float32
BF16 = jnp.bfloat16
MESH = pl.DeviceIdType.MESH
X, Y, Z = 8, 128, 128
SLOTS, CLOUD, BASE = 64, 8, 32
ROWS = CLOUD * X
CHUNKS = 4
PER = SLOTS // CHUNKS
TOP = 8
SLOPE, GROWTH, FLOOR, MASS, LATENT, BUOYANCY = 0.01, 25.0, 0.0625, 0.0004, 200.0, 0.5


def split(x):
    high = x.astype(BF16)
    return high, (x - high.astype(F32)).astype(BF16)


def mm(a, b):
    return jnp.dot(a, b, preferred_element_type=F32)


def times(x, high, low):
    xh, xl = split(x)
    rows = x.shape[0]
    both = mm(jnp.concatenate([xh, xl], axis=0), high)
    return both[:rows] + (both[rows:] + mm(xh, low))


def solve(forcing, explicit, high, low):
    both = times(jnp.concatenate([forcing, explicit], axis=1), high, low)
    return both[:, :Z], explicit + both[:, Z:]


OWN = slice(TOP, TOP + Y)


def move_east(p, e_in, e_out, planes):
    for a in planes:
        e_out[a] = e_in[a] - 0.5 * (p[a + 2, OWN, :] - p[a, OWN, :])


def move_north(p, n, first, last):
    for i in range(X):
        n[i, first:last, :] = n[i, first:last, :] - 0.5 * (
            p[i + 2, first + 1 : last + 1, :] - p[i + 2, first - 1 : last - 1, :]
        )


def explicit_pressure(p, east, west, n, c, i):
    spread = 0.5 * (
        (east - west) + (n[i, TOP + 1 : TOP + Y + 1, :] - n[i, TOP - 1 : TOP + Y - 1, :])
    )
    return p[i + 2, OWN, :] - c * spread


def edges_north(p, n):
    move_north(p, n, TOP - 1, TOP)
    move_north(p, n, TOP, TOP + 8)
    move_north(p, n, TOP + Y - 8, TOP + Y)
    move_north(p, n, TOP + Y, TOP + Y + 1)


def column_matrix(c):
    k = lax.broadcasted_iota(jnp.int32, (Z, Z), 0)
    j = lax.broadcasted_iota(jnp.int32, (Z, Z), 1)
    here = jnp.broadcast_to(c, (Z, Z))
    above = pltpu.roll(here, Z - 1, 1)
    m = jnp.where(k == j, 1.0 + jnp.where(k < Z - 1, here + above, 0.0), 0.0)
    m = m - jnp.where((j == k + 1) & (j < Z - 1), here, 0.0)
    m = m - jnp.where((j == k - 1) & (k < Z - 1), above, 0.0)
    eye = jnp.where(k == j, 1.0, 0.0)
    return eye, m


def column_tables(inverse, c):
    k = lax.broadcasted_iota(jnp.int32, (Z, Z), 0)
    a = jnp.where(k < Z - 1, inverse, 0.0)
    b = a - pltpu.roll(a, 1, 0)
    left = jnp.concatenate([a, b], axis=0)
    j = lax.broadcasted_iota(jnp.int32, (2 * Z, Z), 1)
    m = jnp.where(j < Z - 1, left, 0.0)
    right = (pltpu.roll(m, 1, 1) - m) * c
    return split(jnp.concatenate([left, right], axis=1))


def far_first(count):
    return sorted(range(1, count), key=lambda d: -min(d, count - d))


def kernel_main(
    lo_size,
    e_hbm, n_hbm, v_hbm, p_hbm, th_hbm, hu_hbm, c_hbm, r_hbm, m_hbm, k_hbm,
    p2, e, n, f, th, hu, r, wh, wl, v_new, p_new, total,
    p0, p1, v, c_ref, m_ref, k_ref, cl, xr, a_ref, alone, spill, th_high, th_low, r1, r2, r3,
    load_sem, r_sem, m_sem, hs, hr, as_, ar, z_sem,
):
    gx, gy = lax.axis_index("gx"), lax.axis_index("gy")
    nx, ny = lax.axis_size("gx"), lax.axis_size("gy")
    hi_size = nx // lo_size
    lo, hi = lax.rem(gx, lo_size), gx // lo_size
    right, left = lax.rem(gx + 1, nx), lax.rem(gx + nx - 1, nx)
    up, down = lax.rem(gy + 1, ny), lax.rem(gy + ny - 1, ny)

    barrier = pltpu.get_barrier_semaphore()
    lo_peers = [(hi * lo_size + lax.rem(lo + d, lo_size), gy) for d in far_first(lo_size)]
    hi_peers = [(lax.rem(hi + d, hi_size) * lo_size + lo, gy) for d in far_first(hi_size)]
    gy_peers = [(gx, lax.rem(gy + d, ny)) for d in far_first(ny)]
    relay = ny == 8
    gy_near = [(gx, lax.rem(gy + d, ny)) for d in (1, 2, 6, 7)] if relay else gy_peers
    gy_two = [(gx, lax.rem(gy + d, ny)) for d in (2, 6)] if relay else []
    everyone = gy_near + hi_peers + lo_peers + [(left, gy), (right, gy)]
    for who in everyone:
        pl.semaphore_signal(barrier, inc=1, device_id=who, device_id_type=MESH)
    def droplets(q):
        part = pl.ds(q * PER, PER)
        return (
            pltpu.make_async_copy(r_hbm.at[part], r.at[part], r_sem.at[q]),
            pltpu.make_async_copy(m_hbm.at[part], m_ref.at[part], m_sem.at[q]),
        )

    pairs = (
        (c_hbm, c_ref),
        (th_hbm, th),
        (hu_hbm, hu),
        (k_hbm, k_ref),
        (p_hbm, p0.at[2:10, OWN, :]),
        (e_hbm, e.at[1:9]),
        (n_hbm, n.at[:, OWN, :]),
        (v_hbm, v),
    )
    loads = [
        pltpu.make_async_copy(src, dst, load_sem.at[at]) for at, (src, dst) in enumerate(pairs)
    ]
    for copy in loads[:4]:
        copy.start()
    for q in range(CHUNKS):
        for copy in droplets(q):
            copy.start()
        if q == 0:
            for copy in loads[4:6]:
                copy.start()
    for copy in loads[6:]:
        copy.start()

    loads[0].wait()
    c = c_ref[...]
    eye, m = column_matrix(c)
    half = 0.5 * (3.0 * eye - m)
    xr[0:Z, :] = (6.0 * eye - m) * (1.0 / 7.0)
    xr[Z:, :] = (2.0 * times(half, *split(half)) - eye) * (2.0 / 7.0)

    def square(_, carry):
        x = xr[...]
        high, low = split(x[Z:])
        product = times(x, high, low)
        xr[0:Z, :] = x[:Z] + product[:Z]
        xr[Z:, :] = product[Z:]
        return carry

    lax.fori_loop(0, 4, square, 0)
    high, low = column_tables(xr[0:Z, :], c)
    wh[...] = high
    wl[...] = low

    loads[1].wait()
    loads[2].wait()
    for i in range(X):
        sat = hu[i] * jnp.exp(-SLOPE * th[i]) - 1.0
        cl[:, i : i + 1, :] = GROWTH * jnp.transpose(sat)[BASE : BASE + CLOUD].reshape(CLOUD, 1, Y)

    for copy in loads[4:6]:
        copy.wait()
    a_ref[0] = e[1] - 0.5 * p0[3, OWN, :]
    a_ref[1] = e[8] + 0.5 * p0[8, OWN, :]

    pl.semaphore_wait(barrier, len(everyone))

    def send(src, dst, at, who):
        return pltpu.make_async_remote_copy(
            src_ref=src,
            dst_ref=dst,
            send_sem=hs.at[at],
            recv_sem=hr.at[at],
            device_id=who,
            device_id_type=MESH,
        )

    def exchange(p, outer, at):
        return [
            send(outer[0], p.at[10:11, OWN, :], at, (left, gy)),
            send(outer[1], p.at[1:2, OWN, :], at + 1, (right, gy)),
            send(outer[2], p.at[11:12, OWN, :], at + 2, (left, gy)),
            send(outer[3], p.at[0:1, OWN, :], at + 3, (right, gy)),
            send(p.at[2:10, TOP : TOP + 8, :], p.at[2:10, TOP + Y :, :], at + 4, (gx, down)),
            send(p.at[2:10, TOP + Y - 8 : TOP + Y, :], p.at[2:10, 0:TOP, :], at + 5, (gx, up)),
        ]

    halo0 = [
        send(p_hbm.at[0:1], p0.at[10:11, OWN, :], 0, (left, gy)),
        send(p_hbm.at[7:8], p0.at[1:2, OWN, :], 1, (right, gy)),
        send(a_ref.at[0:1], e.at[9:10], 2, (left, gy)),
        send(a_ref.at[1:2], e.at[0:1], 3, (right, gy)),
        send(p_hbm.at[:, 0:8, :], p0.at[2:10, TOP + Y :, :], 4, (gx, down)),
        send(p_hbm.at[:, Y - 8 :, :], p0.at[2:10, 0:TOP, :], 5, (gx, up)),
        send(n_hbm.at[:, 0:8, :], n.at[:, TOP + Y :, :], 6, (gx, down)),
        send(n_hbm.at[:, Y - 8 :, :], n.at[:, 0:TOP, :], 7, (gx, up)),
    ]
    for copy in halo0[:2] + halo0[4:] + halo0[2:4]:
        copy.start()
    for who in gy_two:
        pl.semaphore_signal(z_sem, inc=1, device_id=who, device_id_type=MESH)
    halo1 = exchange(p1, [alone.at[i : i + 1] for i in range(4)], 8)
    halo2 = exchange(p2, [p2.at[a : a + 1, OWN, :] for a in (2, 9, 3, 8)], 14)

    loads[3].wait()

    def condense(q, acc):
        for copy in droplets(q):
            copy.wait()
        growth = cl[...].reshape(ROWS, Y)
        count = k_ref[...].reshape(ROWS, Y)
        for s in range(PER):
            slot = q * PER + s
            old = r[slot]
            grown = jnp.maximum(old + growth, FLOOR)
            live = count > slot
            mass = m_ref[slot].astype(F32) * (
                grown * grown * lax.rsqrt(grown) - old * old * lax.rsqrt(old)
            )
            r[slot] = jnp.where(live, grown, 0.0)
            acc = acc + jnp.where(live, mass, 0.0)
        return acc

    acc = lax.fori_loop(0, CHUNKS, condense, jnp.zeros((ROWS, Y), F32))
    cl[...] = (MASS * acc).reshape(CLOUD, X, Y)

    zero = jnp.zeros((8, Z), F32)
    percents, warms = zero, zero
    for i in range(X):
        change = cl[:, i : i + 1, :].reshape(CLOUD, Y)
        added = jnp.transpose(
            jnp.concatenate(
                [jnp.zeros((BASE, Y), F32), change, jnp.zeros((Z - BASE - CLOUD, Y), F32)], axis=0
            )
        )
        wet = hu[i] - added
        warm = th[i] + LATENT * added
        hu[i] = wet
        th[i] = warm
        percent = 100.0 * (wet * jnp.exp(-SLOPE * warm) - 1.0)
        percents = percents + jnp.sum(percent.reshape(Y // 8, 8, Z), axis=0)
        warms = warms + jnp.sum(warm.reshape(Y // 8, 8, Z), axis=0)
    row = lax.broadcasted_iota(jnp.int32, (8, Z), 0)

    def gather(buffer, me, who, at):
        return [
            pltpu.make_async_remote_copy(
                src_ref=buffer.at[me],
                dst_ref=buffer.at[me],
                send_sem=as_.at[at + d],
                recv_sem=ar.at[at + d],
                device_id=peer,
                device_id_type=MESH,
            )
            for d, peer in enumerate(who)
        ]

    def add(buffer, count):
        value = buffer[0]
        for d in range(1, count):
            value = value + buffer[d]
        return value

    stage1 = gather(r1, lo, lo_peers, 0)
    stage2 = gather(r2, hi, hi_peers, len(lo_peers))
    stage3 = gather(r3, gy, gy_peers, len(lo_peers) + len(hi_peers))
    r1[lo] = jnp.where(
        row == 0,
        jnp.sum(percents, axis=0, keepdims=True),
        jnp.where(row == 1, jnp.sum(warms, axis=0, keepdims=True), 0.0),
    )
    for copy in stage1:
        copy.start()

    for copy in loads[6:]:
        copy.wait()

    def planes(p, p_next, which, last):
        forcing = jnp.concatenate([v[a] + BUOYANCY * th[a] for a in which], axis=0)
        q = jnp.concatenate(
            [explicit_pressure(p, e[a + 2], e[a], n, c, a) for a in which], axis=0
        )
        vertical, pressure = solve(forcing, q, wh[...], wl[...])
        for at, a in enumerate(which):
            rows = slice(at * Y, (at + 1) * Y)
            p_next[a + 2, OWN, :] = pressure[rows]
            if last:
                f[a] = vertical[rows] + BUOYANCY * th[a]
            else:
                v[a] = vertical[rows]

    def inside(p):
        move_east(p, e, e, range(2, 8))
        move_north(p, n, TOP + 8, TOP + Y - 8)

    def north_edges(p, halo):
        for copy in halo[4:]:
            copy.wait()
        edges_north(p, n)

    inside(p0)
    north_edges(p0, halo0)
    e[1] = e[1] - 0.5 * p0[3, OWN, :]
    e[8] = e[8] + 0.5 * p0[8, OWN, :]

    def by_itself(which, at):
        forcing = jnp.concatenate([v[a] + BUOYANCY * th[a] for a in which], axis=0)
        q = []
        for a in which:
            west = -0.5 * p0[2, OWN, :] if a == 0 else e[a]
            east = 0.5 * p0[9, OWN, :] if a == 7 else e[a + 2]
            q.append(explicit_pressure(p0, east, west, n, c, a))
        vertical, pressure = solve(forcing, jnp.concatenate(q, axis=0), wh[...], wl[...])
        for i, a in enumerate(which):
            v[a] = vertical[i * Y : (i + 1) * Y]
            alone[at + i] = pressure[i * Y : (i + 1) * Y]
            halo1[at + i].start()

    by_itself((0, 7), 0)
    by_itself((1, 6), 2)
    planes(p0, p1, (2, 3, 4, 5), False)

    def added_pressure(planes_of_q):
        q = jnp.concatenate(planes_of_q, axis=0)
        both = times(q, wh[Z:, :], wl[Z:, :])
        return both[:, :Z], q + both[:, Z:]

    quarter, half_c = 0.25 * c, 0.5 * c
    _, pressure = added_pressure(
        [
            quarter * p0[2, OWN, :],
            -half_c * a_ref[0],
            half_c * a_ref[1],
            quarter * p0[9, OWN, :],
        ]
    )
    spill[...] = pressure.reshape(4, Y, Z)

    for copy in halo0[:4]:
        copy.wait()
    vertical, pressure = added_pressure(
        [half_c * e[0], -half_c * e[9], quarter * p0[1, OWN, :], quarter * p0[10, OWN, :]]
    )
    for i, a in enumerate((0, 7, 1, 6)):
        v[a] = v[a] + vertical[i * Y : (i + 1) * Y]
        p1[a + 2, OWN, :] = alone[i] + pressure[i * Y : (i + 1) * Y]
    halo1[4].start()
    halo1[5].start()
    e[0] = e[0] - 0.5 * p0[2, OWN, :]
    e[1] = e[1] + 0.5 * p0[1, OWN, :]
    e[8] = e[8] - 0.5 * p0[10, OWN, :]
    e[9] = e[9] + 0.5 * p0[9, OWN, :]

    for copy in stage1:
        copy.wait()
    r2[hi] = add(r1, lo_size)
    for copy in stage2:
        copy.start()

    eye_v, eye_p = solve(eye, jnp.zeros((Z, Z), F32), wh[...], wl[...])
    eye_v, eye_p = solve(eye + eye_v, eye_p, wh[...], wl[...])
    eye_v, eye_p = solve(eye + eye_v, eye_p, wh[...], wl[...])
    high, low = split(-BUOYANCY * jnp.concatenate([eye_v, eye_p], axis=1))
    th_high[...] = high
    th_low[...] = low

    inside(p1)
    north_edges(p1, halo1)
    for copy in halo1[:4]:
        copy.wait()
    e[0] = e[0] - 0.5 * (p1[2, OWN, :] - (p1[0, OWN, :] + spill[0]))
    e[1] = e[1] - 0.5 * (p1[3, OWN, :] - (p1[1, OWN, :] + spill[1]))
    e[8] = e[8] - 0.5 * ((p1[10, OWN, :] + spill[2]) - p1[8, OWN, :])
    e[9] = e[9] - 0.5 * ((p1[11, OWN, :] + spill[3]) - p1[9, OWN, :])
    planes(p1, p2, (0, 7), True)
    halo2[0].start()
    halo2[1].start()
    planes(p1, p2, (1, 6), True)
    for copy in halo2[2:4]:
        copy.start()

    for copy in stage2:
        copy.wait()
    r3[gy] = add(r2, hi_size)
    if relay:
        pl.semaphore_wait(z_sem, len(gy_two))
    for copy in stage3:
        copy.start()
    planes(p1, p2, (2, 3, 4, 5), True)
    for copy in halo2[4:]:
        copy.start()

    inside(p2)
    north_edges(p2, halo2)
    which = (2, 3, 4, 5)
    forcing = jnp.concatenate([f[a] for a in which], axis=0)
    q = jnp.concatenate([explicit_pressure(p2, e[a + 2], e[a], n, c, a) for a in which], axis=0)
    inner_v, inner_p = solve(forcing, q, wh[...], wl[...])
    v_new[...] = inner_v.reshape(4, Y, Z)
    p_new[...] = inner_p.reshape(4, Y, Z)

    for copy in stage3:
        copy.wait()
    mean = add(r3, ny) * (1.0 / (nx * X * ny * Y))
    pull = times(jnp.concatenate([mean, mean], axis=0), th_high[...], th_low[...])[1:2, :]
    v_new[...] = v_new[...] + pull[:, :Z]
    p_new[...] = p_new[...] + pull[:, Z:]
    total[...] = jnp.where(row == 0, mean, jnp.where(row == 1, pull[:, :Z], pull[:, Z:]))
    for copy in halo2[:4]:
        copy.wait()


def kernel_last(
    p, e, n, f, th, hu, r, wh, wl, v_in, p_in, total, c_ref,
    e_out, n_out, v_out, p_out, th_out, hu_out, r_out, s_out,
    e_new, v_new, p_new, sem,
):
    copies = []

    def out(src, dst):
        copy = pltpu.make_async_copy(src, dst, sem.at[len(copies)])
        copy.start()
        copies.append(copy)

    out(r, r_out)
    out(th, th_out)
    out(hu, hu_out)
    out(n.at[:, OWN, :], n_out)
    out(e.at[2:8], e_out.at[1:7])
    out(v_in, v_out.at[2:6])
    out(p_in, p_out.at[2:6])
    c = c_ref[...]
    stats = total[...]
    s_out[...] = stats[0:1, :]
    for at, a in enumerate((0, 1, 8, 9)):
        e_new[at] = e[a] - 0.5 * (p[a + 2, OWN, :] - p[a, OWN, :])
    out(e_new.at[1:2], e_out.at[0:1])
    out(e_new.at[2:3], e_out.at[7:8])
    forcing = jnp.concatenate([f[0], f[1], f[6], f[7]], axis=0)
    q = jnp.concatenate(
        [
            explicit_pressure(p, e[2], e_new[0], n, c, 0),
            explicit_pressure(p, e[3], e_new[1], n, c, 1),
            explicit_pressure(p, e_new[2], e[6], n, c, 6),
            explicit_pressure(p, e_new[3], e[7], n, c, 7),
        ],
        axis=0,
    )
    vertical, pressure = solve(forcing, q, wh[...], wl[...])
    v_new[...] = (vertical + stats[1:2, :]).reshape(4, Y, Z)
    p_new[...] = (pressure + stats[2:3, :]).reshape(4, Y, Z)
    out(v_new.at[0:2], v_out.at[0:2])
    out(p_new.at[0:2], p_out.at[0:2])
    out(v_new.at[2:4], v_out.at[6:8])
    out(p_new.at[2:4], p_out.at[6:8])
    for copy in copies:
        copy.wait()


def local(lo_size, nx, ny, e, n, v, p, th, hu, sound_speed, radius, multiplicity, count):
    c = sound_speed.reshape(1, Z)
    radius = radius.reshape(SLOTS, ROWS, Y)
    multiplicity = multiplicity.reshape(SLOTS, ROWS, Y)
    stay = pltpu.with_memory_space_constraint
    hbm = pl.BlockSpec(memory_space=pltpu.HBM)
    vmem = pl.BlockSpec(memory_space=pltpu.VMEM)
    dma = pltpu.SemaphoreType.DMA
    peers = lo_size + nx // lo_size + ny - 3
    handed = [
        ((X + 4, Y + 16, Z), F32),
        ((X + 2, Y, Z), F32),
        ((X, Y + 16, Z), F32),
        ((X, Y, Z), F32),
        ((X, Y, Z), F32),
        ((X, Y, Z), F32),
        ((SLOTS, ROWS, Y), F32),
        ((2 * Z, 2 * Z), BF16),
        ((2 * Z, 2 * Z), BF16),
        ((4, Y, Z), F32),
        ((4, Y, Z), F32),
        ((8, Z), F32),
    ]
    state = pl.pallas_call(
        functools.partial(kernel_main, lo_size),
        out_shape=tuple(pltpu.VMEM(s, d) for s, d in handed),
        in_specs=[hbm] * 10,
        out_specs=tuple([vmem] * len(handed)),
        scratch_shapes=[
            pltpu.VMEM((X + 4, Y + 16, Z), F32),
            pltpu.VMEM((X + 4, Y + 16, Z), F32),
            pltpu.VMEM((X, Y, Z), F32),
            pltpu.VMEM((1, Z), F32),
            pltpu.VMEM((SLOTS, ROWS, Y), BF16),
            pltpu.VMEM((CLOUD, X, Y), jnp.int32),
            pltpu.VMEM((CLOUD, X, Y), F32),
            pltpu.VMEM((2 * Z, Z), F32),
            pltpu.VMEM((2, Y, Z), F32),
            pltpu.VMEM((4, Y, Z), F32),
            pltpu.VMEM((4, Y, Z), F32),
            pltpu.VMEM((Z, 2 * Z), BF16),
            pltpu.VMEM((Z, 2 * Z), BF16),
            pltpu.VMEM((lo_size, 8, Z), F32),
            pltpu.VMEM((nx // lo_size, 8, Z), F32),
            pltpu.VMEM((ny, 8, Z), F32),
            dma((8,)),
            dma((CHUNKS,)),
            dma((CHUNKS,)),
            dma((20,)),
            dma((20,)),
            dma((peers,)),
            dma((peers,)),
            pltpu.SemaphoreType.REGULAR,
        ],
        compiler_params=pltpu.CompilerParams(
            collective_id=0, has_side_effects=True, vmem_limit_bytes=24 << 20
        ),
        name="condense_and_step",
    )(*(stay(x, pltpu.HBM) for x in (e, n, v, p, th, hu, c, radius, multiplicity, count)))
    grid = jax.ShapeDtypeStruct((X, Y, Z), F32)
    outs = pl.pallas_call(
        kernel_last,
        out_shape=(
            (grid,) * 6
            + (
                jax.ShapeDtypeStruct((SLOTS, ROWS, Y), F32),
                jax.ShapeDtypeStruct((1, Z), F32),
            )
        ),
        in_specs=[vmem] * (len(handed) + 1),
        out_specs=tuple([hbm] * 7 + [vmem]),
        scratch_shapes=[
            pltpu.VMEM((4, Y, Z), F32),
            pltpu.VMEM((4, Y, Z), F32),
            pltpu.VMEM((4, Y, Z), F32),
            dma((13,)),
        ],
        compiler_params=pltpu.CompilerParams(vmem_limit_bytes=24 << 20),
        name="last_step",
    )(*state, c)
    return outs[:6] + (outs[6].reshape(SLOTS, CLOUD, X, Y), outs[7].reshape(Z))


def solution(mesh):
    nx, ny = mesh.shape["gx"], mesh.shape["gy"]
    lo_size = 8 if nx % 8 == 0 else 2
    grid = P("gx", "gy", None)
    drops = P(None, None, "gx", "gy")
    return jax.shard_map(
        functools.partial(local, lo_size, nx, ny),
        mesh=mesh,
        in_specs=(grid,) * 6 + (P(), drops, drops, P(None, "gx", "gy")),
        out_specs=(grid,) * 6 + (drops, P()),
        check_vma=False,
    )
```

```python
import functools

import jax
import jax.numpy as jnp
from jax import lax
from jax.experimental import pallas as pl
from jax.experimental.pallas import tpu as pltpu
from jax.sharding import PartitionSpec as P

F32 = jnp.float32
BF16 = jnp.bfloat16
MESH = pl.DeviceIdType.MESH
X, Y, Z = 8, 128, 128
SLOTS, CLOUD, BASE = 64, 8, 32
ROWS = CLOUD * X
CHUNKS = 4
PER = SLOTS // CHUNKS
TOP = 8
SLOPE, GROWTH, FLOOR, MASS, LATENT, BUOYANCY = 0.01, 25.0, 0.0625, 0.0004, 200.0, 0.5


def split(x):
    high = x.astype(BF16)
    return high, (x - high.astype(F32)).astype(BF16)


def mm(a, b):
    return jnp.dot(a, b, preferred_element_type=F32)


def times(x, high, low):
    xh, xl = split(x)
    rows = x.shape[0]
    both = mm(jnp.concatenate([xh, xl], axis=0), high)
    return both[:rows] + (both[rows:] + mm(xh, low))


def solve(forcing, explicit, high, low):
    both = times(jnp.concatenate([forcing, explicit], axis=1), high, low)
    return both[:, :Z], explicit + both[:, Z:]


OWN = slice(TOP, TOP + Y)


def move_east(p, e_in, e_out, planes):
    for a in planes:
        e_out[a] = e_in[a] - 0.5 * (p[a + 2, OWN, :] - p[a, OWN, :])


def move_north(p, n, first, last):
    for i in range(X):
        n[i, first:last, :] = n[i, first:last, :] - 0.5 * (
            p[i + 2, first + 1 : last + 1, :] - p[i + 2, first - 1 : last - 1, :]
        )


def explicit_pressure(p, east, west, n, c, i, first=0, last=Y):
    low, high = TOP + first, TOP + last
    spread = 0.5 * ((east - west) + (n[i, low + 1 : high + 1, :] - n[i, low - 1 : high - 1, :]))
    return p[i + 2, low:high, :] - c * spread


def edges_north(p, n):
    move_north(p, n, TOP - 1, TOP + 1)
    move_north(p, n, TOP + Y - 1, TOP + Y + 1)


def pack_rows(p, rows):
    for side, first in enumerate((TOP, TOP + Y - 2)):
        for i in range(2):
            rows[side, i] = p[2 : X + 2, first + i : first + i + 1, :].reshape(X, Z)


def unpack_rows(rows, p):
    for side, first in enumerate((TOP + Y, TOP - 2)):
        for i in range(2):
            p[2 : X + 2, first + i : first + i + 1, :] = rows[side, i].reshape(X, 1, Z)


def column_matrix(c):
    k = lax.broadcasted_iota(jnp.int32, (Z, Z), 0)
    j = lax.broadcasted_iota(jnp.int32, (Z, Z), 1)
    here = jnp.broadcast_to(c, (Z, Z))
    above = pltpu.roll(here, Z - 1, 1)
    m = jnp.where(k == j, 1.0 + jnp.where(k < Z - 1, here + above, 0.0), 0.0)
    m = m - jnp.where((j == k + 1) & (j < Z - 1), here, 0.0)
    m = m - jnp.where((j == k - 1) & (k < Z - 1), above, 0.0)
    eye = jnp.where(k == j, 1.0, 0.0)
    return eye, m


def column_tables(inverse, c):
    k = lax.broadcasted_iota(jnp.int32, (Z, Z), 0)
    a = jnp.where(k < Z - 1, inverse, 0.0)
    b = a - pltpu.roll(a, 1, 0)
    left = jnp.concatenate([a, b], axis=0)
    j = lax.broadcasted_iota(jnp.int32, (2 * Z, Z), 1)
    m = jnp.where(j < Z - 1, left, 0.0)
    right = (pltpu.roll(m, 1, 1) - m) * c
    return split(jnp.concatenate([left, right], axis=1))


def far_first(count):
    return sorted(range(1, count), key=lambda d: -min(d, count - d))


def kernel_main(
    lo_size,
    e_hbm, n_hbm, v_hbm, p_hbm, th_hbm, hu_hbm, c_hbm, r_hbm, m_hbm, k_hbm,
    p2, e, n, f, th, hu, r, wh, wl, v_new, p_new, total,
    p0, p1, v, c_ref, m_ref, k_ref, cl, xr, a_ref, alone, spill, rows_out, rows_in, th_high, th_low, r1, r2, r3,
    load_sem, r_sem, m_sem, hs, hr, as_, ar, z_sem,
):
    gx, gy = lax.axis_index("gx"), lax.axis_index("gy")
    nx, ny = lax.axis_size("gx"), lax.axis_size("gy")
    hi_size = nx // lo_size
    lo, hi = lax.rem(gx, lo_size), gx // lo_size
    right, left = lax.rem(gx + 1, nx), lax.rem(gx + nx - 1, nx)
    up, down = lax.rem(gy + 1, ny), lax.rem(gy + ny - 1, ny)

    barrier = pltpu.get_barrier_semaphore()
    lo_peers = [(hi * lo_size + lax.rem(lo + d, lo_size), gy) for d in far_first(lo_size)]
    hi_peers = [(lax.rem(hi + d, hi_size) * lo_size + lo, gy) for d in far_first(hi_size)]
    gy_peers = [(gx, lax.rem(gy + d, ny)) for d in far_first(ny)]
    relay = ny == 8
    gy_near = [(gx, lax.rem(gy + d, ny)) for d in (1, 2, 6, 7)] if relay else gy_peers
    gy_two = [(gx, lax.rem(gy + d, ny)) for d in (2, 6)] if relay else []
    everyone = gy_near + hi_peers + lo_peers + [(left, gy), (right, gy)]
    for who in everyone:
        pl.semaphore_signal(barrier, inc=1, device_id=who, device_id_type=MESH)
    def droplets(q):
        part = pl.ds(q * PER, PER)
        return (
            pltpu.make_async_copy(r_hbm.at[part], r.at[part], r_sem.at[q]),
            pltpu.make_async_copy(m_hbm.at[part], m_ref.at[part], m_sem.at[q]),
        )

    pairs = (
        (c_hbm, c_ref),
        (th_hbm, th),
        (hu_hbm, hu),
        (k_hbm, k_ref),
        (p_hbm, p0.at[2:10, OWN, :]),
        (e_hbm, e.at[1:9]),
        (n_hbm, n.at[:, OWN, :]),
        (v_hbm, v),
    )
    loads = [
        pltpu.make_async_copy(src, dst, load_sem.at[at]) for at, (src, dst) in enumerate(pairs)
    ]
    for copy in loads[:4]:
        copy.start()
    for q in range(CHUNKS):
        for copy in droplets(q):
            copy.start()
        if q == 0:
            for copy in loads[4:6]:
                copy.start()
    for copy in loads[6:]:
        copy.start()

    loads[0].wait()
    c = c_ref[...]
    eye, m = column_matrix(c)
    half = 0.5 * (3.0 * eye - m)
    xr[0:Z, :] = (6.0 * eye - m) * (1.0 / 7.0)
    xr[Z:, :] = (2.0 * times(half, *split(half)) - eye) * (2.0 / 7.0)

    def square(_, carry):
        x = xr[...]
        high, low = split(x[Z:])
        product = times(x, high, low)
        xr[0:Z, :] = x[:Z] + product[:Z]
        xr[Z:, :] = product[Z:]
        return carry

    lax.fori_loop(0, 4, square, 0)
    high, low = column_tables(xr[0:Z, :], c)
    wh[...] = high
    wl[...] = low

    loads[1].wait()
    loads[2].wait()
    for i in range(X):
        sat = hu[i] * jnp.exp(-SLOPE * th[i]) - 1.0
        cl[:, i : i + 1, :] = GROWTH * jnp.transpose(sat)[BASE : BASE + CLOUD].reshape(CLOUD, 1, Y)

    for copy in loads[4:6]:
        copy.wait()
    a_ref[0] = e[1] - 0.5 * p0[3, OWN, :]
    a_ref[1] = e[8] + 0.5 * p0[8, OWN, :]

    pack_rows(p0, rows_out.at[0])
    pl.semaphore_wait(barrier, len(everyone))

    def send(src, dst, at, who):
        return pltpu.make_async_remote_copy(
            src_ref=src,
            dst_ref=dst,
            send_sem=hs.at[at],
            recv_sem=hr.at[at],
            device_id=who,
            device_id_type=MESH,
        )

    def rows_of(k, at):
        return [
            send(rows_out.at[k, 0], rows_in.at[k, 0], at, (gx, down)),
            send(rows_out.at[k, 1], rows_in.at[k, 1], at + 1, (gx, up)),
        ]

    def exchange(p, k, outer, at):
        return [
            send(outer[0], p.at[10:11, OWN, :], at, (left, gy)),
            send(outer[1], p.at[1:2, OWN, :], at + 1, (right, gy)),
            send(outer[2], p.at[11:12, OWN, :], at + 2, (left, gy)),
            send(outer[3], p.at[0:1, OWN, :], at + 3, (right, gy)),
        ] + rows_of(k, at + 4)

    halo0 = [
        send(p_hbm.at[0:1], p0.at[10:11, OWN, :], 0, (left, gy)),
        send(p_hbm.at[7:8], p0.at[1:2, OWN, :], 1, (right, gy)),
        send(a_ref.at[0:1], e.at[9:10], 2, (left, gy)),
        send(a_ref.at[1:2], e.at[0:1], 3, (right, gy)),
        send(n_hbm.at[:, 0:8, :], n.at[:, TOP + Y :, :], 6, (gx, down)),
        send(n_hbm.at[:, Y - 8 :, :], n.at[:, 0:TOP, :], 7, (gx, up)),
    ] + rows_of(0, 4)
    for copy in halo0[:2] + halo0[4:] + halo0[2:4]:
        copy.start()
    for who in gy_two:
        pl.semaphore_signal(z_sem, inc=1, device_id=who, device_id_type=MESH)
    halo2 = exchange(p2, 2, [p2.at[a : a + 1, OWN, :] for a in (2, 9, 3, 8)], 18)
    halo1 = [
        send(alone.at[i : i + 1, 8 : Y - 8, :], p1.at[to : to + 1, TOP + 8 : TOP + Y - 8, :], at, who)
        for at, (i, to, who) in enumerate(
            ((0, 10, (left, gy)), (3, 1, (right, gy)), (1, 11, (left, gy)), (2, 0, (right, gy))), 8
        )
    ]
    halo1 += rows_of(1, 12)
    halo1 += [
        send(
            alone.at[i : i + 2, row : row + 8, :],
            p1.at[to : to + 2, TOP + row : TOP + row + 8, :],
            at,
            who,
        )
        for at, (i, to, row, who) in enumerate(
            (
                (0, 10, 0, (left, gy)),
                (2, 0, 0, (right, gy)),
                (0, 10, Y - 8, (left, gy)),
                (2, 0, Y - 8, (right, gy)),
            ),
            14,
        )
    ]

    loads[3].wait()

    def condense(q, acc):
        for copy in droplets(q):
            copy.wait()
        growth = cl[...].reshape(ROWS, Y)
        count = k_ref[...].reshape(ROWS, Y)
        for s in range(PER):
            slot = q * PER + s
            old = r[slot]
            grown = jnp.maximum(old + growth, FLOOR)
            live = count > slot
            mass = m_ref[slot].astype(F32) * (
                grown * grown * lax.rsqrt(grown) - old * old * lax.rsqrt(old)
            )
            r[slot] = jnp.where(live, grown, 0.0)
            acc = acc + jnp.where(live, mass, 0.0)
        return acc

    acc = lax.fori_loop(0, CHUNKS, condense, jnp.zeros((ROWS, Y), F32))
    cl[...] = (MASS * acc).reshape(CLOUD, X, Y)

    zero = jnp.zeros((8, Z), F32)
    percents, warms = zero, zero
    for i in range(X):
        change = cl[:, i : i + 1, :].reshape(CLOUD, Y)
        added = jnp.transpose(
            jnp.concatenate(
                [jnp.zeros((BASE, Y), F32), change, jnp.zeros((Z - BASE - CLOUD, Y), F32)], axis=0
            )
        )
        wet = hu[i] - added
        warm = th[i] + LATENT * added
        hu[i] = wet
        th[i] = warm
        percent = 100.0 * (wet * jnp.exp(-SLOPE * warm) - 1.0)
        percents = percents + jnp.sum(percent.reshape(Y // 8, 8, Z), axis=0)
        warms = warms + jnp.sum(warm.reshape(Y // 8, 8, Z), axis=0)
    row = lax.broadcasted_iota(jnp.int32, (8, Z), 0)

    def gather(buffer, me, who, at):
        return [
            pltpu.make_async_remote_copy(
                src_ref=buffer.at[me],
                dst_ref=buffer.at[me],
                send_sem=as_.at[at + d],
                recv_sem=ar.at[at + d],
                device_id=peer,
                device_id_type=MESH,
            )
            for d, peer in enumerate(who)
        ]

    def add(buffer, count):
        value = buffer[0]
        for d in range(1, count):
            value = value + buffer[d]
        return value

    stage1 = gather(r1, lo, lo_peers, 0)
    stage2 = gather(r2, hi, hi_peers, len(lo_peers))
    stage3 = gather(r3, gy, gy_peers, len(lo_peers) + len(hi_peers))
    r1[lo] = jnp.where(
        row == 0,
        jnp.sum(percents, axis=0, keepdims=True),
        jnp.where(row == 1, jnp.sum(warms, axis=0, keepdims=True), 0.0),
    )
    for copy in stage1:
        copy.start()

    for copy in loads[6:]:
        copy.wait()

    def planes(p, p_next, which, last):
        forcing = jnp.concatenate([v[a] + BUOYANCY * th[a] for a in which], axis=0)
        q = jnp.concatenate(
            [explicit_pressure(p, e[a + 2], e[a], n, c, a) for a in which], axis=0
        )
        vertical, pressure = solve(forcing, q, wh[...], wl[...])
        for at, a in enumerate(which):
            rows = slice(at * Y, (at + 1) * Y)
            p_next[a + 2, OWN, :] = pressure[rows]
            if last:
                f[a] = vertical[rows] + BUOYANCY * th[a]
            else:
                v[a] = vertical[rows]

    def inside(p):
        move_east(p, e, e, range(2, 8))
        move_north(p, n, TOP + 1, TOP + Y - 1)

    def north_edges(p, k, copies):
        for copy in copies:
            copy.wait()
        unpack_rows(rows_in.at[k], p)
        edges_north(p, n)

    inside(p0)
    e[1] = e[1] - 0.5 * p0[3, OWN, :]
    e[8] = e[8] + 0.5 * p0[8, OWN, :]
    slot = {0: 0, 1: 1, 6: 2, 7: 3}

    def by_itself(parts):
        forcing = [v[a, low:high] + BUOYANCY * th[a, low:high] for a, low, high in parts]
        q = []
        for a, low, high in parts:
            rows = slice(TOP + low, TOP + high)
            west = -0.5 * p0[2, rows, :] if a == 0 else e[a, low:high]
            east = 0.5 * p0[9, rows, :] if a == 7 else e[a + 2, low:high]
            q.append(explicit_pressure(p0, east, west, n, c, a, low, high))
        vertical, pressure = solve(
            jnp.concatenate(forcing, axis=0), jnp.concatenate(q, axis=0), wh[...], wl[...]
        )
        at = 0
        for a, low, high in parts:
            v[a, low:high] = vertical[at : at + high - low]
            alone[slot[a], low:high] = pressure[at : at + high - low]
            at += high - low

    by_itself([(a, 8, Y - 8) for a in (0, 7)])
    halo1[0].start()
    halo1[1].start()
    by_itself([(a, 8, Y - 8) for a in (1, 6)])
    halo1[2].start()
    halo1[3].start()
    north_edges(p0, 0, halo0[4:])
    by_itself([(a, low, low + 8) for a in (0, 1, 6, 7) for low in (0, Y - 8)])
    for copy in halo1[6:]:
        copy.start()
    planes(p0, p1, (2, 3, 4, 5), False)

    def added_pressure(planes_of_q):
        q = jnp.concatenate(planes_of_q, axis=0)
        both = times(q, wh[Z:, :], wl[Z:, :])
        return both[:, :Z], q + both[:, Z:]

    quarter, half_c = 0.25 * c, 0.5 * c
    _, pressure = added_pressure(
        [
            quarter * p0[2, OWN, :],
            -half_c * a_ref[0],
            half_c * a_ref[1],
            quarter * p0[9, OWN, :],
        ]
    )
    spill[...] = pressure.reshape(4, Y, Z)

    for copy in halo0[:4]:
        copy.wait()
    vertical, pressure = added_pressure(
        [half_c * e[0], -half_c * e[9], quarter * p0[1, OWN, :], quarter * p0[10, OWN, :]]
    )
    for i, a in enumerate((0, 7, 1, 6)):
        v[a] = v[a] + vertical[i * Y : (i + 1) * Y]
        p1[a + 2, OWN, :] = alone[slot[a]] + pressure[i * Y : (i + 1) * Y]
    pack_rows(p1, rows_out.at[1])
    halo1[4].start()
    halo1[5].start()
    e[0] = e[0] - 0.5 * p0[2, OWN, :]
    e[1] = e[1] + 0.5 * p0[1, OWN, :]
    e[8] = e[8] - 0.5 * p0[10, OWN, :]
    e[9] = e[9] + 0.5 * p0[9, OWN, :]

    for copy in stage1:
        copy.wait()
    r2[hi] = add(r1, lo_size)
    for copy in stage2:
        copy.start()

    eye_v, eye_p = solve(eye, jnp.zeros((Z, Z), F32), wh[...], wl[...])
    eye_v, eye_p = solve(eye + eye_v, eye_p, wh[...], wl[...])
    eye_v, eye_p = solve(eye + eye_v, eye_p, wh[...], wl[...])
    high, low = split(-BUOYANCY * jnp.concatenate([eye_v, eye_p], axis=1))
    th_high[...] = high
    th_low[...] = low

    inside(p1)
    north_edges(p1, 1, halo1[4:6])
    for copy in halo1[:4] + halo1[6:]:
        copy.wait()
    e[0] = e[0] - 0.5 * (p1[2, OWN, :] - (p1[0, OWN, :] + spill[0]))
    e[1] = e[1] - 0.5 * (p1[3, OWN, :] - (p1[1, OWN, :] + spill[1]))
    e[8] = e[8] - 0.5 * ((p1[10, OWN, :] + spill[2]) - p1[8, OWN, :])
    e[9] = e[9] - 0.5 * ((p1[11, OWN, :] + spill[3]) - p1[9, OWN, :])
    planes(p1, p2, (0, 7), True)
    halo2[0].start()
    halo2[1].start()
    planes(p1, p2, (1, 6), True)
    for copy in halo2[2:4]:
        copy.start()

    for copy in stage2:
        copy.wait()
    r3[gy] = add(r2, hi_size)
    if relay:
        pl.semaphore_wait(z_sem, len(gy_two))
    for copy in stage3:
        copy.start()
    planes(p1, p2, (2, 3, 4, 5), True)
    pack_rows(p2, rows_out.at[2])
    for copy in halo2[4:]:
        copy.start()

    inside(p2)
    north_edges(p2, 2, halo2[4:])
    which = (2, 3, 4, 5)
    forcing = jnp.concatenate([f[a] for a in which], axis=0)
    q = jnp.concatenate([explicit_pressure(p2, e[a + 2], e[a], n, c, a) for a in which], axis=0)
    inner_v, inner_p = solve(forcing, q, wh[...], wl[...])
    v_new[...] = inner_v.reshape(4, Y, Z)
    p_new[...] = inner_p.reshape(4, Y, Z)

    for copy in stage3:
        copy.wait()
    mean = add(r3, ny) * (1.0 / (nx * X * ny * Y))
    pull = times(jnp.concatenate([mean, mean], axis=0), th_high[...], th_low[...])[1:2, :]
    v_new[...] = v_new[...] + pull[:, :Z]
    p_new[...] = p_new[...] + pull[:, Z:]
    total[...] = jnp.where(row == 0, mean, jnp.where(row == 1, pull[:, :Z], pull[:, Z:]))
    for copy in halo2[:4]:
        copy.wait()


def kernel_last(
    p, e, n, f, th, hu, r, wh, wl, v_in, p_in, total, c_ref,
    e_out, n_out, v_out, p_out, th_out, hu_out, r_out, s_out,
    e_new, v_new, p_new, sem,
):
    copies = []

    def out(src, dst):
        copy = pltpu.make_async_copy(src, dst, sem.at[len(copies)])
        copy.start()
        copies.append(copy)

    out(r, r_out)
    out(th, th_out)
    out(hu, hu_out)
    out(n.at[:, OWN, :], n_out)
    out(e.at[2:8], e_out.at[1:7])
    out(v_in, v_out.at[2:6])
    out(p_in, p_out.at[2:6])
    c = c_ref[...]
    stats = total[...]
    s_out[...] = stats[0:1, :]
    for at, a in enumerate((0, 1, 8, 9)):
        e_new[at] = e[a] - 0.5 * (p[a + 2, OWN, :] - p[a, OWN, :])
    out(e_new.at[1:2], e_out.at[0:1])
    out(e_new.at[2:3], e_out.at[7:8])
    forcing = jnp.concatenate([f[0], f[1], f[6], f[7]], axis=0)
    q = jnp.concatenate(
        [
            explicit_pressure(p, e[2], e_new[0], n, c, 0),
            explicit_pressure(p, e[3], e_new[1], n, c, 1),
            explicit_pressure(p, e_new[2], e[6], n, c, 6),
            explicit_pressure(p, e_new[3], e[7], n, c, 7),
        ],
        axis=0,
    )
    vertical, pressure = solve(forcing, q, wh[...], wl[...])
    v_new[...] = (vertical + stats[1:2, :]).reshape(4, Y, Z)
    p_new[...] = (pressure + stats[2:3, :]).reshape(4, Y, Z)
    out(v_new.at[0:2], v_out.at[0:2])
    out(p_new.at[0:2], p_out.at[0:2])
    out(v_new.at[2:4], v_out.at[6:8])
    out(p_new.at[2:4], p_out.at[6:8])
    for copy in copies:
        copy.wait()


def local(lo_size, nx, ny, e, n, v, p, th, hu, sound_speed, radius, multiplicity, count):
    c = sound_speed.reshape(1, Z)
    radius = radius.reshape(SLOTS, ROWS, Y)
    multiplicity = multiplicity.reshape(SLOTS, ROWS, Y)
    stay = pltpu.with_memory_space_constraint
    hbm = pl.BlockSpec(memory_space=pltpu.HBM)
    vmem = pl.BlockSpec(memory_space=pltpu.VMEM)
    dma = pltpu.SemaphoreType.DMA
    peers = lo_size + nx // lo_size + ny - 3
    handed = [
        ((X + 4, Y + 16, Z), F32),
        ((X + 2, Y, Z), F32),
        ((X, Y + 16, Z), F32),
        ((X, Y, Z), F32),
        ((X, Y, Z), F32),
        ((X, Y, Z), F32),
        ((SLOTS, ROWS, Y), F32),
        ((2 * Z, 2 * Z), BF16),
        ((2 * Z, 2 * Z), BF16),
        ((4, Y, Z), F32),
        ((4, Y, Z), F32),
        ((8, Z), F32),
    ]
    state = pl.pallas_call(
        functools.partial(kernel_main, lo_size),
        out_shape=tuple(pltpu.VMEM(s, d) for s, d in handed),
        in_specs=[hbm] * 10,
        out_specs=tuple([vmem] * len(handed)),
        scratch_shapes=[
            pltpu.VMEM((X + 4, Y + 16, Z), F32),
            pltpu.VMEM((X + 4, Y + 16, Z), F32),
            pltpu.VMEM((X, Y, Z), F32),
            pltpu.VMEM((1, Z), F32),
            pltpu.VMEM((SLOTS, ROWS, Y), BF16),
            pltpu.VMEM((CLOUD, X, Y), jnp.int32),
            pltpu.VMEM((CLOUD, X, Y), F32),
            pltpu.VMEM((2 * Z, Z), F32),
            pltpu.VMEM((2, Y, Z), F32),
            pltpu.VMEM((4, Y, Z), F32),
            pltpu.VMEM((4, Y, Z), F32),
            pltpu.VMEM((3, 2, 2, X, Z), F32),
            pltpu.VMEM((3, 2, 2, X, Z), F32),
            pltpu.VMEM((Z, 2 * Z), BF16),
            pltpu.VMEM((Z, 2 * Z), BF16),
            pltpu.VMEM((lo_size, 8, Z), F32),
            pltpu.VMEM((nx // lo_size, 8, Z), F32),
            pltpu.VMEM((ny, 8, Z), F32),
            dma((8,)),
            dma((CHUNKS,)),
            dma((CHUNKS,)),
            dma((24,)),
            dma((24,)),
            dma((peers,)),
            dma((peers,)),
            pltpu.SemaphoreType.REGULAR,
        ],
        compiler_params=pltpu.CompilerParams(
            collective_id=0, has_side_effects=True, vmem_limit_bytes=24 << 20
        ),
        name="condense_and_step",
    )(*(stay(x, pltpu.HBM) for x in (e, n, v, p, th, hu, c, radius, multiplicity, count)))
    grid = jax.ShapeDtypeStruct((X, Y, Z), F32)
    outs = pl.pallas_call(
        kernel_last,
        out_shape=(
            (grid,) * 6
            + (
                jax.ShapeDtypeStruct((SLOTS, ROWS, Y), F32),
                jax.ShapeDtypeStruct((1, Z), F32),
            )
        ),
        in_specs=[vmem] * (len(handed) + 1),
        out_specs=tuple([hbm] * 7 + [vmem]),
        scratch_shapes=[
            pltpu.VMEM((4, Y, Z), F32),
            pltpu.VMEM((4, Y, Z), F32),
            pltpu.VMEM((4, Y, Z), F32),
            dma((13,)),
        ],
        compiler_params=pltpu.CompilerParams(vmem_limit_bytes=24 << 20),
        name="last_step",
    )(*state, c)
    return outs[:6] + (outs[6].reshape(SLOTS, CLOUD, X, Y), outs[7].reshape(Z))


def solution(mesh):
    nx, ny = mesh.shape["gx"], mesh.shape["gy"]
    lo_size = 8 if nx % 8 == 0 else 2
    grid = P("gx", "gy", None)
    drops = P(None, None, "gx", "gy")
    return jax.shard_map(
        functools.partial(local, lo_size, nx, ny),
        mesh=mesh,
        in_specs=(grid,) * 6 + (P(), drops, drops, P(None, "gx", "gy")),
        out_specs=(grid,) * 6 + (drops, P()),
        check_vma=False,
    )
```

```python
import functools

import jax
import jax.numpy as jnp
from jax import lax
from jax.experimental import pallas as pl
from jax.experimental.pallas import tpu as pltpu
from jax.sharding import PartitionSpec as P

F32 = jnp.float32
BF16 = jnp.bfloat16
MESH = pl.DeviceIdType.MESH
X, Y, Z = 8, 128, 128
SLOTS, CLOUD, BASE = 64, 8, 32
ROWS = CLOUD * X
CHUNKS = 4
PER = SLOTS // CHUNKS
TOP = 8
SLOPE, GROWTH, FLOOR, MASS, LATENT, BUOYANCY = 0.01, 25.0, 0.0625, 0.0004, 200.0, 0.5


def split(x):
    high = x.astype(BF16)
    return high, (x - high.astype(F32)).astype(BF16)


def mm(a, b):
    return jnp.dot(a, b, preferred_element_type=F32)


def times(x, high, low):
    xh, xl = split(x)
    rows = x.shape[0]
    both = mm(jnp.concatenate([xh, xl], axis=0), high)
    return both[:rows] + (both[rows:] + mm(xh, low))


def solve(forcing, explicit, high, low):
    both = times(jnp.concatenate([forcing, explicit], axis=1), high, low)
    return both[:, :Z], explicit + both[:, Z:]


OWN = slice(TOP, TOP + Y)


def move_east(p, e_in, e_out, planes):
    for a in planes:
        e_out[a] = e_in[a] - 0.5 * (p[a + 2, OWN, :] - p[a, OWN, :])


def move_north(p, n, first, last):
    for i in range(X):
        n[i, first:last, :] = n[i, first:last, :] - 0.5 * (
            p[i + 2, first + 1 : last + 1, :] - p[i + 2, first - 1 : last - 1, :]
        )


def explicit_pressure(p, east, west, n, c, i, first=0, last=Y):
    low, high = TOP + first, TOP + last
    spread = 0.5 * ((east - west) + (n[i, low + 1 : high + 1, :] - n[i, low - 1 : high - 1, :]))
    return p[i + 2, low:high, :] - c * spread


def edges_north(p, n):
    move_north(p, n, TOP - 1, TOP + 1)
    move_north(p, n, TOP + Y - 1, TOP + Y + 1)


def pack_rows(p, rows):
    for side, first in enumerate((TOP, TOP + Y - 2)):
        for i in range(2):
            rows[side, i] = p[2 : X + 2, first + i : first + i + 1, :].reshape(X, Z)


def unpack_rows(rows, p):
    for side, first in enumerate((TOP + Y, TOP - 2)):
        for i in range(2):
            p[2 : X + 2, first + i : first + i + 1, :] = rows[side, i].reshape(X, 1, Z)


def column_matrix(c):
    k = lax.broadcasted_iota(jnp.int32, (Z, Z), 0)
    j = lax.broadcasted_iota(jnp.int32, (Z, Z), 1)
    here = jnp.broadcast_to(c, (Z, Z))
    above = pltpu.roll(here, Z - 1, 1)
    m = jnp.where(k == j, 1.0 + jnp.where(k < Z - 1, here + above, 0.0), 0.0)
    m = m - jnp.where((j == k + 1) & (j < Z - 1), here, 0.0)
    m = m - jnp.where((j == k - 1) & (k < Z - 1), above, 0.0)
    eye = jnp.where(k == j, 1.0, 0.0)
    return eye, m


def column_tables(inverse, c):
    k = lax.broadcasted_iota(jnp.int32, (Z, Z), 0)
    a = jnp.where(k < Z - 1, inverse, 0.0)
    b = a - pltpu.roll(a, 1, 0)
    left = jnp.concatenate([a, b], axis=0)
    j = lax.broadcasted_iota(jnp.int32, (2 * Z, Z), 1)
    m = jnp.where(j < Z - 1, left, 0.0)
    right = (pltpu.roll(m, 1, 1) - m) * c
    return split(jnp.concatenate([left, right], axis=1))


def far_first(count):
    return sorted(range(1, count), key=lambda d: -min(d, count - d))


def kernel_main(
    lo_size,
    e_hbm, n_hbm, v_hbm, p_hbm, th_hbm, hu_hbm, c_hbm, r_hbm, m_hbm, k_hbm,
    p2, e, n, f, th, hu, r, wh, wl, v_new, p_new, total, th_high, th_low,
    p0, p1, v, c_ref, m_ref, k_ref, cl, xr, a_ref, alone, spill, rows_out, rows_in, r1, r2, r3,
    load_sem, r_sem, m_sem, hs, hr, as_, ar, z_sem,
):
    gx, gy = lax.axis_index("gx"), lax.axis_index("gy")
    nx, ny = lax.axis_size("gx"), lax.axis_size("gy")
    hi_size = nx // lo_size
    lo, hi = lax.rem(gx, lo_size), gx // lo_size
    right, left = lax.rem(gx + 1, nx), lax.rem(gx + nx - 1, nx)
    up, down = lax.rem(gy + 1, ny), lax.rem(gy + ny - 1, ny)

    barrier = pltpu.get_barrier_semaphore()
    lo_peers = [(hi * lo_size + lax.rem(lo + d, lo_size), gy) for d in far_first(lo_size)]
    hi_peers = [(lax.rem(hi + d, hi_size) * lo_size + lo, gy) for d in far_first(hi_size)]
    gy_peers = [(gx, lax.rem(gy + d, ny)) for d in far_first(ny)]
    relay = ny == 8
    gy_near = [(gx, lax.rem(gy + d, ny)) for d in (1, 2, 6, 7)] if relay else gy_peers
    gy_two = [(gx, lax.rem(gy + d, ny)) for d in (2, 6)] if relay else []
    everyone = gy_near + hi_peers + lo_peers + [(left, gy), (right, gy)]
    for who in everyone:
        pl.semaphore_signal(barrier, inc=1, device_id=who, device_id_type=MESH)
    def droplets(q):
        part = pl.ds(q * PER, PER)
        return (
            pltpu.make_async_copy(r_hbm.at[part], r.at[part], r_sem.at[q]),
            pltpu.make_async_copy(m_hbm.at[part], m_ref.at[part], m_sem.at[q]),
        )

    pairs = (
        (c_hbm, c_ref),
        (th_hbm, th),
        (hu_hbm, hu),
        (k_hbm, k_ref),
        (p_hbm, p0.at[2:10, OWN, :]),
        (e_hbm, e.at[1:9]),
        (n_hbm, n.at[:, OWN, :]),
        (v_hbm, v),
    )
    loads = [
        pltpu.make_async_copy(src, dst, load_sem.at[at]) for at, (src, dst) in enumerate(pairs)
    ]
    for copy in loads[:4]:
        copy.start()
    for q in range(CHUNKS):
        for copy in droplets(q):
            copy.start()
        if q == 0:
            for copy in loads[4:6]:
                copy.start()
    for copy in loads[6:]:
        copy.start()

    loads[0].wait()
    c = c_ref[...]
    eye, m = column_matrix(c)
    half = 0.5 * (3.0 * eye - m)
    xr[0:Z, :] = (6.0 * eye - m) * (1.0 / 7.0)
    xr[Z:, :] = (2.0 * times(half, *split(half)) - eye) * (2.0 / 7.0)

    def square(_, carry):
        x = xr[...]
        high, low = split(x[Z:])
        product = times(x, high, low)
        xr[0:Z, :] = x[:Z] + product[:Z]
        xr[Z:, :] = product[Z:]
        return carry

    lax.fori_loop(0, 4, square, 0)
    high, low = column_tables(xr[0:Z, :], c)
    wh[...] = high
    wl[...] = low

    loads[1].wait()
    loads[2].wait()
    for i in range(X):
        sat = hu[i] * jnp.exp(-SLOPE * th[i]) - 1.0
        cl[:, i : i + 1, :] = GROWTH * jnp.transpose(sat)[BASE : BASE + CLOUD].reshape(CLOUD, 1, Y)

    for copy in loads[4:6]:
        copy.wait()
    a_ref[0] = e[1] - 0.5 * p0[3, OWN, :]
    a_ref[1] = e[8] + 0.5 * p0[8, OWN, :]

    pack_rows(p0, rows_out.at[0])
    pl.semaphore_wait(barrier, len(everyone))

    def send(src, dst, at, who):
        return pltpu.make_async_remote_copy(
            src_ref=src,
            dst_ref=dst,
            send_sem=hs.at[at],
            recv_sem=hr.at[at],
            device_id=who,
            device_id_type=MESH,
        )

    def rows_of(k, at):
        return [
            send(rows_out.at[k, 0], rows_in.at[k, 0], at, (gx, down)),
            send(rows_out.at[k, 1], rows_in.at[k, 1], at + 1, (gx, up)),
        ]

    def exchange(p, k, outer, at):
        return [
            send(outer[0], p.at[10:11, OWN, :], at, (left, gy)),
            send(outer[1], p.at[1:2, OWN, :], at + 1, (right, gy)),
            send(outer[2], p.at[11:12, OWN, :], at + 2, (left, gy)),
            send(outer[3], p.at[0:1, OWN, :], at + 3, (right, gy)),
        ] + rows_of(k, at + 4)

    halo0 = [
        send(p_hbm.at[0:1], p0.at[10:11, OWN, :], 0, (left, gy)),
        send(p_hbm.at[7:8], p0.at[1:2, OWN, :], 1, (right, gy)),
        send(a_ref.at[0:1], e.at[9:10], 2, (left, gy)),
        send(a_ref.at[1:2], e.at[0:1], 3, (right, gy)),
        send(n_hbm.at[:, 0:8, :], n.at[:, TOP + Y :, :], 6, (gx, down)),
        send(n_hbm.at[:, Y - 8 :, :], n.at[:, 0:TOP, :], 7, (gx, up)),
    ] + rows_of(0, 4)
    for copy in halo0[:2] + halo0[4:] + halo0[2:4]:
        copy.start()
    for who in gy_two:
        pl.semaphore_signal(z_sem, inc=1, device_id=who, device_id_type=MESH)
    halo2 = exchange(p2, 2, [p2.at[a : a + 1, OWN, :] for a in (2, 9, 3, 8)], 18)
    halo1 = [
        send(alone.at[i : i + 1, 8 : Y - 8, :], p1.at[to : to + 1, TOP + 8 : TOP + Y - 8, :], at, who)
        for at, (i, to, who) in enumerate(
            ((0, 10, (left, gy)), (3, 1, (right, gy)), (1, 11, (left, gy)), (2, 0, (right, gy))), 8
        )
    ]
    halo1 += rows_of(1, 12)
    halo1 += [
        send(
            alone.at[i : i + 2, row : row + 8, :],
            p1.at[to : to + 2, TOP + row : TOP + row + 8, :],
            at,
            who,
        )
        for at, (i, to, row, who) in enumerate(
            (
                (0, 10, 0, (left, gy)),
                (2, 0, 0, (right, gy)),
                (0, 10, Y - 8, (left, gy)),
                (2, 0, Y - 8, (right, gy)),
            ),
            14,
        )
    ]

    loads[3].wait()

    def condense(q, acc):
        for copy in droplets(q):
            copy.wait()
        growth = cl[...].reshape(ROWS, Y)
        count = k_ref[...].reshape(ROWS, Y)
        for s in range(PER):
            slot = q * PER + s
            old = r[slot]
            grown = jnp.maximum(old + growth, FLOOR)
            live = count > slot
            mass = m_ref[slot].astype(F32) * (
                grown * grown * lax.rsqrt(grown) - old * old * lax.rsqrt(old)
            )
            r[slot] = jnp.where(live, grown, 0.0)
            acc = acc + jnp.where(live, mass, 0.0)
        return acc

    acc = lax.fori_loop(0, CHUNKS, condense, jnp.zeros((ROWS, Y), F32))
    cl[...] = (MASS * acc).reshape(CLOUD, X, Y)

    zero = jnp.zeros((8, Z), F32)
    percents, warms = zero, zero
    for i in range(X):
        change = cl[:, i : i + 1, :].reshape(CLOUD, Y)
        added = jnp.transpose(
            jnp.concatenate(
                [jnp.zeros((BASE, Y), F32), change, jnp.zeros((Z - BASE - CLOUD, Y), F32)], axis=0
            )
        )
        wet = hu[i] - added
        warm = th[i] + LATENT * added
        hu[i] = wet
        th[i] = warm
        percent = 100.0 * (wet * jnp.exp(-SLOPE * warm) - 1.0)
        percents = percents + jnp.sum(percent.reshape(Y // 8, 8, Z), axis=0)
        warms = warms + jnp.sum(warm.reshape(Y // 8, 8, Z), axis=0)
    row = lax.broadcasted_iota(jnp.int32, (8, Z), 0)

    def gather(buffer, me, who, at):
        return [
            pltpu.make_async_remote_copy(
                src_ref=buffer.at[me],
                dst_ref=buffer.at[me],
                send_sem=as_.at[at + d],
                recv_sem=ar.at[at + d],
                device_id=peer,
                device_id_type=MESH,
            )
            for d, peer in enumerate(who)
        ]

    def add(buffer, count):
        value = buffer[0]
        for d in range(1, count):
            value = value + buffer[d]
        return value

    stage1 = gather(r1, lo, lo_peers, 0)
    stage2 = gather(r2, hi, hi_peers, len(lo_peers))
    stage3 = gather(r3, gy, gy_peers, len(lo_peers) + len(hi_peers))
    r1[lo] = jnp.where(
        row == 0,
        jnp.sum(percents, axis=0, keepdims=True),
        jnp.where(row == 1, jnp.sum(warms, axis=0, keepdims=True), 0.0),
    )
    for copy in stage1:
        copy.start()

    for copy in loads[6:]:
        copy.wait()

    def planes(p, p_next, which, last):
        forcing = jnp.concatenate([v[a] + BUOYANCY * th[a] for a in which], axis=0)
        q = jnp.concatenate(
            [explicit_pressure(p, e[a + 2], e[a], n, c, a) for a in which], axis=0
        )
        vertical, pressure = solve(forcing, q, wh[...], wl[...])
        for at, a in enumerate(which):
            rows = slice(at * Y, (at + 1) * Y)
            p_next[a + 2, OWN, :] = pressure[rows]
            if last:
                f[a] = vertical[rows] + BUOYANCY * th[a]
            else:
                v[a] = vertical[rows]

    def inside(p):
        move_east(p, e, e, range(2, 8))
        move_north(p, n, TOP + 1, TOP + Y - 1)

    def north_edges(p, k, copies):
        for copy in copies:
            copy.wait()
        unpack_rows(rows_in.at[k], p)
        edges_north(p, n)

    inside(p0)
    e[1] = e[1] - 0.5 * p0[3, OWN, :]
    e[8] = e[8] + 0.5 * p0[8, OWN, :]
    slot = {0: 0, 1: 1, 6: 2, 7: 3}

    def by_itself(parts):
        forcing = [v[a, low:high] + BUOYANCY * th[a, low:high] for a, low, high in parts]
        q = []
        for a, low, high in parts:
            rows = slice(TOP + low, TOP + high)
            west = -0.5 * p0[2, rows, :] if a == 0 else e[a, low:high]
            east = 0.5 * p0[9, rows, :] if a == 7 else e[a + 2, low:high]
            q.append(explicit_pressure(p0, east, west, n, c, a, low, high))
        vertical, pressure = solve(
            jnp.concatenate(forcing, axis=0), jnp.concatenate(q, axis=0), wh[...], wl[...]
        )
        at = 0
        for a, low, high in parts:
            v[a, low:high] = vertical[at : at + high - low]
            alone[slot[a], low:high] = pressure[at : at + high - low]
            at += high - low

    by_itself([(a, 8, Y - 8) for a in (0, 7)])
    halo1[0].start()
    halo1[1].start()
    by_itself([(a, 8, Y - 8) for a in (1, 6)])
    halo1[2].start()
    halo1[3].start()
    north_edges(p0, 0, halo0[4:])
    by_itself([(a, low, low + 8) for a in (0, 1, 6, 7) for low in (0, Y - 8)])
    for copy in halo1[6:]:
        copy.start()
    planes(p0, p1, (2, 3, 4, 5), False)

    def added_pressure(planes_of_q):
        q = jnp.concatenate(planes_of_q, axis=0)
        both = times(q, wh[Z:, :], wl[Z:, :])
        return both[:, :Z], q + both[:, Z:]

    quarter, half_c = 0.25 * c, 0.5 * c
    _, pressure = added_pressure(
        [
            quarter * p0[2, OWN, :],
            -half_c * a_ref[0],
            half_c * a_ref[1],
            quarter * p0[9, OWN, :],
        ]
    )
    spill[...] = pressure.reshape(4, Y, Z)

    for copy in halo0[:4]:
        copy.wait()
    vertical, pressure = added_pressure(
        [half_c * e[0], -half_c * e[9], quarter * p0[1, OWN, :], quarter * p0[10, OWN, :]]
    )
    for i, a in enumerate((0, 7, 1, 6)):
        v[a] = v[a] + vertical[i * Y : (i + 1) * Y]
        p1[a + 2, OWN, :] = alone[slot[a]] + pressure[i * Y : (i + 1) * Y]
    pack_rows(p1, rows_out.at[1])
    halo1[4].start()
    halo1[5].start()
    e[0] = e[0] - 0.5 * p0[2, OWN, :]
    e[1] = e[1] + 0.5 * p0[1, OWN, :]
    e[8] = e[8] - 0.5 * p0[10, OWN, :]
    e[9] = e[9] + 0.5 * p0[9, OWN, :]

    for copy in stage1:
        copy.wait()
    r2[hi] = add(r1, lo_size)
    for copy in stage2:
        copy.start()

    eye_v, eye_p = solve(eye, jnp.zeros((Z, Z), F32), wh[...], wl[...])
    eye_v, eye_p = solve(eye + eye_v, eye_p, wh[...], wl[...])
    eye_v, eye_p = solve(eye + eye_v, eye_p, wh[...], wl[...])
    high, low = split(-BUOYANCY * jnp.concatenate([eye_v, eye_p], axis=1))
    th_high[...] = high
    th_low[...] = low

    inside(p1)
    north_edges(p1, 1, halo1[4:6])
    for copy in halo1[:4] + halo1[6:]:
        copy.wait()
    e[0] = e[0] - 0.5 * (p1[2, OWN, :] - (p1[0, OWN, :] + spill[0]))
    e[1] = e[1] - 0.5 * (p1[3, OWN, :] - (p1[1, OWN, :] + spill[1]))
    e[8] = e[8] - 0.5 * ((p1[10, OWN, :] + spill[2]) - p1[8, OWN, :])
    e[9] = e[9] - 0.5 * ((p1[11, OWN, :] + spill[3]) - p1[9, OWN, :])
    planes(p1, p2, (0, 7), True)
    halo2[0].start()
    halo2[1].start()
    planes(p1, p2, (1, 6), True)
    for copy in halo2[2:4]:
        copy.start()

    for copy in stage2:
        copy.wait()
    r3[gy] = add(r2, hi_size)
    if relay:
        pl.semaphore_wait(z_sem, len(gy_two))
    for copy in stage3:
        copy.start()
    planes(p1, p2, (2, 3, 4, 5), True)
    pack_rows(p2, rows_out.at[2])
    for copy in halo2[4:]:
        copy.start()

    inside(p2)
    north_edges(p2, 2, halo2[4:])
    which = (2, 3, 4, 5)
    forcing = jnp.concatenate([f[a] for a in which], axis=0)
    q = jnp.concatenate([explicit_pressure(p2, e[a + 2], e[a], n, c, a) for a in which], axis=0)
    inner_v, inner_p = solve(forcing, q, wh[...], wl[...])
    v_new[...] = inner_v.reshape(4, Y, Z)
    p_new[...] = inner_p.reshape(4, Y, Z)

    for copy in stage3:
        copy.wait()
    total[...] = add(r3, ny) * (1.0 / (nx * X * ny * Y))
    for copy in halo2[:4]:
        copy.wait()


def kernel_last(
    p, e, n, f, th, hu, r, wh, wl, v_in, p_in, total, th_high, th_low, c_ref,
    e_out, n_out, v_out, p_out, th_out, hu_out, r_out, s_out,
    e_new, v_new, p_new, v_mid, p_mid, sem,
):
    copies = []

    def out(src, dst):
        copy = pltpu.make_async_copy(src, dst, sem.at[len(copies)])
        copy.start()
        copies.append(copy)

    out(r, r_out)
    out(th, th_out)
    out(hu, hu_out)
    out(n.at[:, OWN, :], n_out)
    out(e.at[2:8], e_out.at[1:7])
    c = c_ref[...]
    mean = total[...]
    s_out[...] = mean[0:1, :]
    pull = times(jnp.concatenate([mean, mean], axis=0), th_high[...], th_low[...])[1:2, :]
    v_mid[...] = v_in[...] + pull[:, :Z]
    p_mid[...] = p_in[...] + pull[:, Z:]
    out(v_mid, v_out.at[2:6])
    out(p_mid, p_out.at[2:6])
    for at, a in enumerate((0, 1, 8, 9)):
        e_new[at] = e[a] - 0.5 * (p[a + 2, OWN, :] - p[a, OWN, :])
    out(e_new.at[1:2], e_out.at[0:1])
    out(e_new.at[2:3], e_out.at[7:8])
    forcing = jnp.concatenate([f[0], f[1], f[6], f[7]], axis=0)
    q = jnp.concatenate(
        [
            explicit_pressure(p, e[2], e_new[0], n, c, 0),
            explicit_pressure(p, e[3], e_new[1], n, c, 1),
            explicit_pressure(p, e_new[2], e[6], n, c, 6),
            explicit_pressure(p, e_new[3], e[7], n, c, 7),
        ],
        axis=0,
    )
    vertical, pressure = solve(forcing, q, wh[...], wl[...])
    v_new[...] = (vertical + pull[:, :Z]).reshape(4, Y, Z)
    p_new[...] = (pressure + pull[:, Z:]).reshape(4, Y, Z)
    out(v_new.at[0:2], v_out.at[0:2])
    out(p_new.at[0:2], p_out.at[0:2])
    out(v_new.at[2:4], v_out.at[6:8])
    out(p_new.at[2:4], p_out.at[6:8])
    for copy in copies:
        copy.wait()


def local(lo_size, nx, ny, e, n, v, p, th, hu, sound_speed, radius, multiplicity, count):
    c = sound_speed.reshape(1, Z)
    radius = radius.reshape(SLOTS, ROWS, Y)
    multiplicity = multiplicity.reshape(SLOTS, ROWS, Y)
    stay = pltpu.with_memory_space_constraint
    hbm = pl.BlockSpec(memory_space=pltpu.HBM)
    vmem = pl.BlockSpec(memory_space=pltpu.VMEM)
    dma = pltpu.SemaphoreType.DMA
    peers = lo_size + nx // lo_size + ny - 3
    handed = [
        ((X + 4, Y + 16, Z), F32),
        ((X + 2, Y, Z), F32),
        ((X, Y + 16, Z), F32),
        ((X, Y, Z), F32),
        ((X, Y, Z), F32),
        ((X, Y, Z), F32),
        ((SLOTS, ROWS, Y), F32),
        ((2 * Z, 2 * Z), BF16),
        ((2 * Z, 2 * Z), BF16),
        ((4, Y, Z), F32),
        ((4, Y, Z), F32),
        ((8, Z), F32),
        ((Z, 2 * Z), BF16),
        ((Z, 2 * Z), BF16),
    ]
    state = pl.pallas_call(
        functools.partial(kernel_main, lo_size),
        out_shape=tuple(pltpu.VMEM(s, d) for s, d in handed),
        in_specs=[hbm] * 10,
        out_specs=tuple([vmem] * len(handed)),
        scratch_shapes=[
            pltpu.VMEM((X + 4, Y + 16, Z), F32),
            pltpu.VMEM((X + 4, Y + 16, Z), F32),
            pltpu.VMEM((X, Y, Z), F32),
            pltpu.VMEM((1, Z), F32),
            pltpu.VMEM((SLOTS, ROWS, Y), BF16),
            pltpu.VMEM((CLOUD, X, Y), jnp.int32),
            pltpu.VMEM((CLOUD, X, Y), F32),
            pltpu.VMEM((2 * Z, Z), F32),
            pltpu.VMEM((2, Y, Z), F32),
            pltpu.VMEM((4, Y, Z), F32),
            pltpu.VMEM((4, Y, Z), F32),
            pltpu.VMEM((3, 2, 2, X, Z), F32),
            pltpu.VMEM((3, 2, 2, X, Z), F32),
            pltpu.VMEM((lo_size, 8, Z), F32),
            pltpu.VMEM((nx // lo_size, 8, Z), F32),
            pltpu.VMEM((ny, 8, Z), F32),
            dma((8,)),
            dma((CHUNKS,)),
            dma((CHUNKS,)),
            dma((24,)),
            dma((24,)),
            dma((peers,)),
            dma((peers,)),
            pltpu.SemaphoreType.REGULAR,
        ],
        compiler_params=pltpu.CompilerParams(
            collective_id=0, has_side_effects=True, vmem_limit_bytes=24 << 20
        ),
        name="condense_and_step",
    )(*(stay(x, pltpu.HBM) for x in (e, n, v, p, th, hu, c, radius, multiplicity, count)))
    grid = jax.ShapeDtypeStruct((X, Y, Z), F32)
    outs = pl.pallas_call(
        kernel_last,
        out_shape=(
            (grid,) * 6
            + (
                jax.ShapeDtypeStruct((SLOTS, ROWS, Y), F32),
                jax.ShapeDtypeStruct((1, Z), F32),
            )
        ),
        in_specs=[vmem] * (len(handed) + 1),
        out_specs=tuple([hbm] * 7 + [vmem]),
        scratch_shapes=[
            pltpu.VMEM((4, Y, Z), F32),
            pltpu.VMEM((4, Y, Z), F32),
            pltpu.VMEM((4, Y, Z), F32),
            pltpu.VMEM((4, Y, Z), F32),
            pltpu.VMEM((4, Y, Z), F32),
            dma((13,)),
        ],
        compiler_params=pltpu.CompilerParams(vmem_limit_bytes=24 << 20),
        name="last_step",
    )(*state, c)
    return outs[:6] + (outs[6].reshape(SLOTS, CLOUD, X, Y), outs[7].reshape(Z))


def solution(mesh):
    nx, ny = mesh.shape["gx"], mesh.shape["gy"]
    lo_size = 8 if nx % 8 == 0 else 2
    grid = P("gx", "gy", None)
    drops = P(None, None, "gx", "gy")
    return jax.shard_map(
        functools.partial(local, lo_size, nx, ny),
        mesh=mesh,
        in_specs=(grid,) * 6 + (P(), drops, drops, P(None, "gx", "gy")),
        out_specs=(grid,) * 6 + (drops, P()),
        check_vma=False,
    )
```
